256 devices in a mesh: lat: 16 (over x, y_hi, core), lon: 16 (over y_lo, z).
Axes of the slice: x: 4, y: 4 (y_hi: 2, y_lo: 2; y = y_hi * 2 + y_lo), z: 8, core: 2. Of those that a mesh axis runs over, the one named last changes fastest.
Arguments:
- obs_values: float32 [30, 8192], P(None, ('lat', 'lon')), may hold values from -6 to 6
- obs_lat: int32 [8192], P(('lat', 'lon')), may hold values from 0 to 255, as said below
- obs_lon: int32 [8192], P(('lat', 'lon')), may hold values from 0 to 4095, as said below
- instrument: int32 [8192], P(('lat', 'lon')), may hold values from 0 to 3
- length_scale: float32 [4], replicated, may hold values from 2 to 32
- w_first: bfloat16 [3, 3, 64, 124], replicated, may hold values from -0.1875 to 0.1875
- b_first: float32 [64], replicated, may hold values from -3 to 3
- w_second: bfloat16 [3, 3, 64, 64], replicated, may hold values from -0.25 to 0.25
- b_second: float32 [64], replicated, may hold values from -3 to 3
Outputs:
- encoded: bfloat16 [64, 256, 4096], P(None, 'lat', 'lon')
The draws below stay inside these ranges and needn't reach their ends.
Inputs may be any that keep to these rules, and one draw needn't show every extreme that they name: `obs_lon`: the rows held by ingest device q (rows q * 32 to (q + 1) * 32 - 1, devices counted with lat slowest and lon fastest) lie in that device's longitude band: columns b * 256 to (b + 1) * 256 - 1, with b the device's lon index. `obs_lat`: the rows held by ingest device q lie in that device's latitude band: rows a * 16 to (a + 1) * 16 - 1, with a the device's lat index.
All inputs are finite; a program needn't handle non-finite values.
Results may differ from the reference program's by a relative error of at most 0.00125.
The reference program's roundings to bfloat16 on the way count: a program that leaves them out, or rounds other values in their place, can miss the bound.
Values may be sent and summed in bfloat16 or wider, within the bound.
No kernel may reach another device: no remote copies, remote signals or barrier semaphores. Data moves between devices by JAX's collectives and lax.ppermute only.
A program may use at most 64 MiB of HBM per device.

```python
import math
import jax
import jax.numpy as jnp
from jax import lax

INSTR = 4
VALUES = 30
CHANNELS = 64
CLAT = 16
CLON = 256
ROWS_DEV = 32
CIN = 124
NLAT = 256
NLON = 4096
ROWS = 8192


def draw_obs_lon(key, part):
    key = jax.random.fold_in(key, 7)
    indices = jnp.arange(ROWS, dtype=jnp.int32)
    band = indices // ROWS_DEV % (NLON // CLON)
    inner = jax.random.randint(key, (ROWS,), 0, CLON, dtype=jnp.int32)
    inner = jnp.where(indices == 0, 0, inner)
    inner = jnp.where(indices == ROWS - 1, CLON - 1, inner)
    return (band * CLON + inner).astype(jnp.int32)


def draw_obs_lat(key, part):
    key = jax.random.fold_in(key, 11)
    indices = jnp.arange(ROWS, dtype=jnp.int32)
    band = indices // ROWS_DEV // (NLON // CLON)
    inner = jax.random.randint(key, (ROWS,), 0, CLAT, dtype=jnp.int32)
    inner = jnp.where(indices == 0, 0, inner)
    inner = jnp.where(indices == ROWS - 1, CLAT - 1, inner)
    return (band * CLAT + inner).astype(jnp.int32)


def set_ends(drawn, stream_key, least, largest):
    extent = drawn.shape
    spot = [jax.random.randint(jax.random.fold_in(stream_key, axis), (), 0, extent[axis]) for axis in range(len(extent))]
    drawn = drawn.at[tuple(spot)].set(least)
    longest = extent.index(max(extent))
    spot[longest] = (spot[longest] + 1) % extent[longest]
    return drawn.at[tuple(spot)].set(largest)


def steps_of(stream_key, shape, shards, low, top_value):
    def one(position, parts):
        heights = jax.random.uniform(jax.random.fold_in(jax.random.fold_in(stream_key, 6), position), (parts,), jnp.float32, low / len(shards), top_value / len(shards))
        return jnp.repeat(jnp.exp(heights), shape[position] // parts).reshape((-1,) + (1,) * (len(shape) - position - 1))

    gain = one(*shards[0])
    for cut in shards[1:]:
        gain = gain * one(*cut)
    return gain


def bell_draw(rng, extent, deviation, most, shards=(), kind=jnp.bfloat16):
    factor_of = steps_of(rng, extent, shards, -0.22, 0.18) if shards else 1.0
    values = jax.random.normal(rng, extent, jnp.float32) * deviation * factor_of
    return jnp.minimum(jnp.maximum(values, -most), most).astype(kind)


def setup_inputs(seed: int = 0) -> dict:
    seeds = jax.random.split(jax.random.key(seed), 10)
    obs_values = bell_draw(seeds[0], (VALUES, ROWS), 1.0, 6.0, ((1, 256),), jnp.float32)
    obs_lat = draw_obs_lat(jax.random.fold_in(seeds[9], 71), 0)
    obs_lon = draw_obs_lon(jax.random.fold_in(seeds[9], 71), 0)
    instrument = set_ends(jax.random.randint(seeds[3], (ROWS,), 0, INSTR), jax.random.fold_in(seeds[3], 1), 0, INSTR - 1).astype(jnp.int32)
    length_scale = jnp.clip(jnp.exp(jax.random.uniform(seeds[4], (INSTR,), jnp.float32, math.log(2.0), math.log(32.0))), 2.0, 32.0)
    w_first = bell_draw(seeds[5], (3, 3, CHANNELS, CIN), (9 * CIN) ** -0.5, 0.1875)
    b_first = bell_draw(seeds[6], (CHANNELS,), 0.5, 3.0, (), jnp.float32)
    w_second = bell_draw(seeds[7], (3, 3, CHANNELS, CHANNELS), (9 * CHANNELS) ** -0.5, 0.25)
    b_second = bell_draw(seeds[8], (CHANNELS,), 0.5, 3.0, (), jnp.float32)
    return {"obs_values": obs_values, "obs_lat": obs_lat, "obs_lon": obs_lon, "instrument": instrument, "length_scale": length_scale, "w_first": w_first, "b_first": b_first, "w_second": w_second, "b_second": b_second}


def row_rate(instrument, length_scale):
    table = 0.5 / (length_scale * length_scale)
    onehot = (instrument[None, :] == jnp.arange(INSTR, dtype=jnp.int32)[:, None]).astype(jnp.float32)
    rate = jnp.sum(onehot * table[:, None], axis=0)
    reach = jnp.sum(onehot * (4.0 * length_scale)[:, None], axis=0)
    return onehot, rate, reach


def row_channels(obs_values, onehot):
    count = obs_values.shape[1]
    augmented = jnp.concatenate([jnp.ones((1, count), jnp.float32), obs_values], axis=0)
    return (onehot[:, None, :] * augmented[None, :, :]).reshape(INSTR * (VALUES + 1), count)


def lon_weights(columns, obs_lon, rate, reach, total):
    offset = jnp.mod(columns[:, None] - obs_lon[None, :], total)
    dist = jnp.minimum(offset, total - offset)
    kernel = jnp.where(dist <= reach[None, :], jnp.exp(-dist * dist * rate[None, :]), 0.0)
    return kernel.astype(jnp.bfloat16)


def features_of(sums):
    shaped = sums.reshape((INSTR, VALUES + 1) + sums.shape[1:])
    density = shaped[:, 0:1]
    result = jnp.concatenate([jnp.log1p(density), shaped[:, 1:] / (1.0 + density)], axis=1)
    return result.reshape(sums.shape).astype(jnp.bfloat16)


def conv_valid(source, weights):
    height = source.shape[1] - 2
    width = source.shape[2] - 2
    total = jnp.zeros((weights.shape[2], height, width), jnp.float32)
    for first in range(3):
        for second in range(3):
            total = total + jnp.einsum("oc,chw->ohw", weights[first, second], source[:, first:first + height, second:second + width], precision=lax.Precision.HIGHEST)
    return total


def pad_grid(source):
    wrapped = jnp.concatenate([source[:, :, -1:], source, source[:, :, :1]], axis=2)
    return jnp.pad(wrapped, ((0, 0), (1, 1), (0, 0)))


def reference(obs_values, obs_lat, obs_lon, instrument, length_scale, w_first, b_first, w_second, b_second):
    onehot, rate, reach = row_rate(instrument, length_scale)
    channels = row_channels(obs_values, onehot)
    columns = jnp.arange(NLON).astype(jnp.float32)
    lon_kernel = lon_weights(columns, obs_lon.astype(jnp.float32), rate, reach, float(NLON)).astype(jnp.float32)
    lat_pos = obs_lat.astype(jnp.float32)

    def one_row(row):
        gap = row - lat_pos
        lat_k = jnp.where(jnp.abs(gap) <= reach, jnp.exp(-(gap * gap) * rate), 0.0)
        weighted = (lat_k[None, :] * channels).astype(jnp.bfloat16).astype(jnp.float32)
        sums = jnp.dot(weighted, lon_kernel.T, precision=lax.Precision.HIGHEST)
        return features_of(sums)

    feats = lax.map(one_row, jnp.arange(NLAT).astype(jnp.float32))
    feats = jnp.transpose(feats, (1, 0, 2)).astype(jnp.float32)
    pre = conv_valid(pad_grid(feats), w_first.astype(jnp.float32)) + b_first[:, None, None]
    hidden = jax.nn.silu(pre).astype(jnp.bfloat16).astype(jnp.float32)
    out = conv_valid(pad_grid(hidden), w_second.astype(jnp.float32)) + b_second[:, None, None]
    return out.astype(jnp.bfloat16)
```

```python
import jax
import jax.numpy as jnp
from jax import lax
from jax.experimental import pallas as pl
from jax.experimental.pallas import tpu as pltpu
from jax.sharding import PartitionSpec as P

CLAT = 16
CLON = 256
INSTR = 4
VALUES = 30
CHANNELS = 64
SLOT = 32
NLAT = 256
NLON = 4096
ROWS_DEV = 32
EXT = CLAT + 4
HID = CLAT + 2
WIDE = 384
BAND = 512
LOG2E = 1.4426950408889634
NT = (((1,), (1,)), ((), ()))
NN = (((1,), (0,)), ((), ()))


def dot(a, b, dims=NN):
    return lax.dot_general(a, b, dims, preferred_element_type=jnp.float32)


def encode_kernel(
    scale_ref, first_ref, minus_ref, own_ref, plus_ref, w1_ref, b1_ref, w2_ref, b2_ref,
    out_ref, wt, la, lb, lc, sa, sb, sc, feat, hid, stage,
):
    lat_first = first_ref[0]
    lon_first = first_ref[1]
    lat_first_f = lat_first.astype(jnp.float32)
    lon_first_f = lon_first.astype(jnp.float32)
    grid_row = lax.broadcasted_iota(jnp.int32, (24, 128), 0) + (lat_first - 2)
    row_ok = (grid_row >= 0) & (grid_row < NLAT)
    grid_row = grid_row.astype(jnp.float32)
    sub = lax.broadcasted_iota(jnp.int32, (128, 128), 0)
    col_a = sub.astype(jnp.float32)
    col_b = (sub + 128).astype(jnp.float32)
    inst_c = ((sub + 16) // 32) % 4
    edge = sub - 32 * inst_c
    edge = jnp.where(edge > 64, edge - 128, edge)
    col_c = jnp.where(edge >= 0, edge + 256, edge).astype(jnp.float32)
    inst_c = inst_c.astype(jnp.float32)

    for part, ref in enumerate((minus_ref, own_ref, plus_ref)):
        for block in range(4):
            at = part * BAND + block * 128
            data = ref[block]
            lat = data[0:1]
            lon = data[31:32]
            inst = data[32:33]
            scale = jnp.zeros_like(lat)
            for k in range(INSTR):
                scale = jnp.where(inst == float(k), scale_ref[k], scale)
            rate = -LOG2E * (0.5 / (scale * scale))
            reach = 4.0 * scale
            rel = lon - lon_first_f
            rel = jnp.where(rel > NLON / 2, rel - NLON, rel)
            rel = jnp.where(rel < -NLON / 2, rel + NLON, rel)
            gap = grid_row - lat
            lat_k = jnp.where(
                (jnp.abs(gap) <= reach) & row_ok, jnp.exp2(gap * gap * rate), 0.0
            )
            which = lax.broadcasted_iota(jnp.int32, (SLOT, 128), 0)
            aug = jnp.where(which == 0, 1.0, jnp.where(which == 31, 0.0, data[0:SLOT]))
            for i in range(EXT):
                wt[i * SLOT : (i + 1) * SLOT, at : at + 128] = (lat_k[i : i + 1] * aug).astype(
                    jnp.bfloat16
                )

            def lon_k(col):
                dist = jnp.abs(col - rel)
                return jnp.where(dist <= reach, jnp.exp2(dist * dist * rate), 0.0)

            for use, col, ref_l, base in (
                (part < 2, col_a, la, at),
                (part > 0, col_b, lb, at - BAND),
            ):
                if use:
                    ker = lon_k(col)
                    for k in range(INSTR):
                        ref_l[k * 128 : (k + 1) * 128, base : base + 128] = jnp.where(
                            inst == float(k), ker, 0.0
                        ).astype(jnp.bfloat16)
            lc[:, at : at + 128] = jnp.where(inst == inst_c, lon_k(col_c), 0.0).astype(
                jnp.bfloat16
            )

    for pair in range(2):
        rows = slice(pair * 256, (pair + 1) * 256)
        sa[:, rows] = dot(wt[:, 0 : 2 * BAND], la[rows, :], NT)
        sb[:, rows] = dot(wt[:, BAND : 3 * BAND], lb[rows, :], NT)
    sc[...] = dot(wt[...], lc[...], NT)

    slot_row = lax.broadcasted_iota(jnp.int32, (SLOT, WIDE), 0)
    for i in range(EXT):
        rows = slice(i * SLOT, (i + 1) * SLOT)
        edges = sc[rows, :]
        for k in range(INSTR):
            lanes = slice(k * 128, (k + 1) * 128)
            edge_k = edges if k == 0 else pltpu.roll(edges, 128 - 32 * k, 1)
            sums = jnp.concatenate([sa[rows, lanes], sb[rows, lanes], edge_k], axis=1)
            density = sums[0:1]
            inverse = 1.0 / (1.0 + density)
            value = jnp.where(slot_row == 0, jnp.log1p(density), sums * inverse)
            feat[i * 128 + k * SLOT : i * 128 + (k + 1) * SLOT, :] = value.astype(jnp.bfloat16)

    w1 = w1_ref[...]
    b1 = b1_ref[...]
    for pair in range(HID // 2):
        h = 2 * pair
        x = jnp.concatenate(
            [feat[h * 128 : (h + 3) * 128, :], feat[(h + 1) * 128 : (h + 4) * 128, :]], axis=1
        )
        y = dot(w1, x)
        for n in range(2):
            lanes = slice(n * WIDE, (n + 1) * WIDE)
            pre = (
                y[64:128, lanes]
                + pltpu.roll(y[0:64, lanes], 1, 1)
                + pltpu.roll(y[128:192, lanes], WIDE - 1, 1)
                + b1
            )
            act = pre / (1.0 + jnp.exp(-pre))
            row = lat_first - 1 + h + n
            if h + n in (0, HID - 1):
                act = jnp.where((row >= 0) & (row < NLAT), act, 0.0)
            hid[(h + n) * 64 : (h + n + 1) * 64, :] = act.astype(jnp.bfloat16)

    w2 = w2_ref[...]
    b2 = b2_ref[...]
    for pair in range(CLAT // 2):
        r = 2 * pair
        x = jnp.concatenate(
            [hid[r * 64 : (r + 3) * 64, :], hid[(r + 1) * 64 : (r + 4) * 64, :]], axis=1
        )
        y = dot(w2, x)
        for n in range(2):
            lanes = slice(n * WIDE, (n + 1) * WIDE)
            total = (
                y[64:128, lanes]
                + pltpu.roll(y[0:64, lanes], 1, 1)
                + pltpu.roll(y[128:192, lanes], WIDE - 1, 1)
            )[:, 0:CLON] + b2
            stage[pl.ds(r + n, CHANNELS, CLAT), :] = total[:, 0:128]
            stage[pl.ds(CHANNELS * CLAT + r + n, CHANNELS, CLAT), :] = total[:, 128:256]
    half = CHANNELS * CLAT
    for n in range(2):
        out_ref[:, :, n * 128 : (n + 1) * 128] = (
            stage[n * half : (n + 1) * half, :].reshape(CHANNELS, CLAT, 128).astype(jnp.bfloat16)
        )


def encode(scale, first, minus, own, plus, w1, b1, w2, b2):
    vmem = pl.BlockSpec(memory_space=pltpu.VMEM)
    smem = pl.BlockSpec(memory_space=pltpu.SMEM)
    bf16, f32 = jnp.bfloat16, jnp.float32
    return pl.pallas_call(
        encode_kernel,
        out_shape=jax.ShapeDtypeStruct((CHANNELS, CLAT, CLON), bf16),
        in_specs=[smem, smem] + [vmem] * 7,
        out_specs=vmem,
        scratch_shapes=[
            pltpu.VMEM((EXT * SLOT, 3 * BAND), bf16),
            pltpu.VMEM((INSTR * 128, 2 * BAND), bf16),
            pltpu.VMEM((INSTR * 128, 2 * BAND), bf16),
            pltpu.VMEM((128, 3 * BAND), bf16),
            pltpu.VMEM((EXT * SLOT, INSTR * 128), f32),
            pltpu.VMEM((EXT * SLOT, INSTR * 128), f32),
            pltpu.VMEM((EXT * SLOT, 128), f32),
            pltpu.VMEM((EXT * 128, WIDE), bf16),
            pltpu.VMEM((HID * CHANNELS, WIDE), bf16),
            pltpu.VMEM((2 * CHANNELS * CLAT, 128), f32),
        ],
        compiler_params=pltpu.CompilerParams(vmem_limit_bytes=48 * 1024 * 1024),
    )(scale, first, minus, own, plus, w1, b1, w2, b2)


def send(array, axis, target):
    peers = lax.axis_size(axis)
    return lax.ppermute(array, axis, [(i, target(i) % peers) for i in range(peers)])


def body(
    obs_values, obs_lat, obs_lon, instrument, length_scale, w_first, b_first, w_second, b_second
):
    f32 = jnp.float32
    rows = jnp.concatenate(
        [
            obs_lat.astype(f32)[None],
            obs_values,
            obs_lon.astype(f32)[None],
            instrument.astype(f32)[None],
            jnp.zeros((7, ROWS_DEV), f32),
        ],
        axis=0,
    )
    rows = jnp.concatenate([rows, send(rows, "lat", lambda i: i ^ 1)], axis=1)
    rows = jnp.concatenate([rows, send(rows, "lat", lambda i: i ^ 2)], axis=1)
    rows = jnp.stack([rows] + [send(rows, "lat", lambda i, k=k: i + 4 * k) for k in (1, 2, 3)])
    minus = send(rows, "lon", lambda i: i + 1)
    plus = send(rows, "lon", lambda i: i - 1)
    first = jnp.stack([lax.axis_index("lat") * CLAT, lax.axis_index("lon") * CLON])
    w1 = jnp.pad(
        w_first.reshape(3, 3, CHANNELS, INSTR, VALUES + 1), ((0, 0),) * 4 + ((0, 1),)
    )
    w1 = jnp.transpose(w1, (1, 2, 0, 3, 4)).reshape(3 * CHANNELS, 3 * INSTR * SLOT)
    w2 = jnp.transpose(w_second, (1, 2, 0, 3)).reshape(3 * CHANNELS, 3 * CHANNELS)
    return encode(
        length_scale, first, minus, rows, plus, w1, b_first[:, None], w2, b_second[:, None]
    )


def solution(mesh):
    return jax.shard_map(
        body,
        mesh=mesh,
        in_specs=(
            P(None, ("lat", "lon")),
            P(("lat", "lon")),
            P(("lat", "lon")),
            P(("lat", "lon")),
            P(),
            P(),
            P(),
            P(),
            P(),
        ),
        out_specs=P(None, "lat", "lon"),
        check_vma=False,
    )
```

```python
import jax
import jax.numpy as jnp
from jax import lax
from jax.experimental import pallas as pl
from jax.experimental.pallas import tpu as pltpu
from jax.sharding import PartitionSpec as P

CLAT = 16
CLON = 256
INSTR = 4
VALUES = 30
CHANNELS = 64
CIN = 124
SLOT = 32
NLAT = 256
NLON = 4096
ROWS_DEV = 32
EXT = CLAT + 4
HID = CLAT + 2
WIDE = 384
BAND = 512
LOG2E = 1.4426950408889634
NT = (((1,), (1,)), ((), ()))
NN = (((1,), (0,)), ((), ()))


def dot(a, b, dims=NN):
    return lax.dot_general(a, b, dims, preferred_element_type=jnp.float32)


def fetch(sources, targets, sems):
    copies = [
        pltpu.make_async_copy(source, target, sems.at[n])
        for n, (source, target) in enumerate(zip(sources, targets, strict=True))
    ]
    for copy in copies:
        copy.start()
    for copy in copies:
        copy.wait()


def weights_kernel(first, second, small, w1, w2, b1, b2, table):
    source = lax.broadcasted_iota(jnp.int32, (CIN, 128), 0)
    slot = lax.broadcasted_iota(jnp.int32, (CIN, 128), 1)
    for k in range(1, INSTR):
        slot = jnp.where(slot == SLOT * k - 1, -1, slot)
    shifted = source
    for k in range(1, INSTR):
        shifted = shifted + jnp.where(source >= k * (VALUES + 1), 1, 0)
    spread = jnp.where(shifted == slot, 1.0, 0.0).astype(jnp.bfloat16)
    for a in range(3):
        for b in range(3):
            rows = slice(b * CHANNELS, (b + 1) * CHANNELS)
            w1[rows, a * 128 : (a + 1) * 128] = dot(first[a, b], spread).astype(jnp.bfloat16)
            w2[rows, a * CHANNELS : (a + 1) * CHANNELS] = second[a, b]
    up = lax.broadcasted_iota(jnp.int32, (CHANNELS, CHANNELS), 0)
    across = lax.broadcasted_iota(jnp.int32, (CHANNELS, CHANNELS), 1)
    for n, column in enumerate((b1, b2)):
        row = small[n : n + 1, 0:CHANNELS]
        column[...] = jnp.sum(jnp.where(up == across, row, 0.0), axis=1, keepdims=True)
    for k in range(INSTR):
        length = small[2:3, k : k + 1]
        reach = jnp.floor(4.0 * length)
        table[k : k + 1] = jnp.broadcast_to(-LOG2E * (0.5 / (length * length)), (1, 128))
        table[INSTR + k : INSTR + k + 1] = jnp.broadcast_to(reach * reach, (1, 128))


def build(ref, part, shift, table, targets, wt, lc):
    lat_first = lax.axis_index("lat") * CLAT
    grid_row = lax.broadcasted_iota(jnp.int32, (24, 128), 0) + (lat_first - 2)
    row_ok = (grid_row >= 0) & (grid_row < NLAT)
    grid_row = grid_row.astype(jnp.float32)
    lane = lax.broadcasted_iota(jnp.int32, (128, 128), 0)
    edge = lax.broadcasted_iota(jnp.int32, (16, 128), 0)
    edge_inst = (edge // 4).astype(jnp.float32)
    edge = edge % 4
    edge_col = (edge - 2 + jnp.where(edge >= 2, CLON, 0)).astype(jnp.float32)
    which = lax.broadcasted_iota(jnp.int32, (SLOT, 128), 0)
    for block in range(4):
        at = part * BAND + block * 128
        data = ref[block]
        lat = data[0:1]
        lon = data[31:32]
        inst = data[32:33]
        rate = table[0:1]
        reach2 = table[INSTR : INSTR + 1]
        for k in range(1, INSTR):
            rate = jnp.where(inst == float(k), table[k : k + 1], rate)
            reach2 = jnp.where(inst == float(k), table[INSTR + k : INSTR + k + 1], reach2)
        rel = (lon.astype(jnp.int32) & (CLON - 1)).astype(jnp.float32) + shift

        def kernel_of(gap):
            gap2 = gap * gap
            return jnp.where(gap2 <= reach2, jnp.exp2(gap2 * rate), 0.0)

        lat_k = jnp.where(row_ok, kernel_of(grid_row - lat), 0.0)
        aug = jnp.where(which == 0, 1.0, jnp.where(which == 31, 0.0, data[0:SLOT]))
        for i in range(EXT):
            wt[i * SLOT : (i + 1) * SLOT, at : at + 128] = (lat_k[i : i + 1] * aug).astype(
                jnp.bfloat16
            )
        chosen = [jnp.where(inst == float(k), 1.0, 0.0).astype(jnp.bfloat16) for k in range(INSTR)]
        for target, start, base in targets:
            ker = kernel_of((lane + start).astype(jnp.float32) - rel).astype(jnp.bfloat16)
            for k in range(INSTR):
                target[k * 128 : (k + 1) * 128, base + block * 128 : base + (block + 1) * 128] = (
                    ker * chosen[k]
                )
        lc[0:16, at : at + 128] = jnp.where(
            inst == edge_inst, kernel_of(edge_col - rel), 0.0
        ).astype(jnp.bfloat16)
        lc[16:128, at : at + 128] = jnp.zeros((112, 128), jnp.bfloat16)


def own_kernel(own_ref, table, sa, sb, sc, wt, la, lb, lc):
    build(own_ref, 0, 0.0, table, ((la, 0, 0), (lb, 128, 0)), wt, lc)
    for pair in range(2):
        rows = slice(pair * 256, (pair + 1) * 256)
        sa[:, rows] = dot(wt[...], la[rows, :], NT)
        sb[:, rows] = dot(wt[...], lb[rows, :], NT)
    sc[...] = dot(wt[...], lc[...], NT)


def encode_kernel(
    minus_ref, plus_ref, table, own_a, own_b, own_c, w1_ref, b1_ref, w2_ref, b2_ref,
    out_ref, wt, la, lb, lc, sa, sb, sc, feat, hid, stage,
):
    lat_first = lax.axis_index("lat") * CLAT
    build(minus_ref, 0, -float(CLON), table, ((la, 0, 0),), wt, lc)
    build(plus_ref, 1, float(CLON), table, ((lb, 128, 0),), wt, lc)

    for pair in range(2):
        rows = slice(pair * 256, (pair + 1) * 256)
        sa[:, rows] = dot(wt[:, 0:BAND], la[rows, :], NT)
        sb[:, rows] = dot(wt[:, BAND : 2 * BAND], lb[rows, :], NT)
    sc[...] = dot(wt[...], lc[...], NT)

    slot_row = lax.broadcasted_iota(jnp.int32, (SLOT, WIDE), 0)
    for i in range(EXT):
        rows = slice(i * SLOT, (i + 1) * SLOT)
        edges = sc[rows, :] + own_c[rows, :]
        for k in range(INSTR):
            lanes = slice(k * 128, (k + 1) * 128)
            sums = jnp.concatenate(
                [
                    sa[rows, lanes] + own_a[rows, lanes],
                    sb[rows, lanes] + own_b[rows, lanes],
                    pltpu.roll(edges, 126 - 4 * k, 1),
                ],
                axis=1,
            )
            density = sums[0:1]
            inverse = 1.0 / (1.0 + density)
            value = jnp.where(slot_row == 0, jnp.log1p(density), sums * inverse)
            feat[i * 128 + k * SLOT : i * 128 + (k + 1) * SLOT, :] = value.astype(jnp.bfloat16)

    w1 = w1_ref[...]
    b1 = b1_ref[...]
    for pair in range(HID // 2):
        h = 2 * pair
        x = jnp.concatenate(
            [feat[h * 128 : (h + 3) * 128, :], feat[(h + 1) * 128 : (h + 4) * 128, :]], axis=1
        )
        y = dot(w1, x)
        for n in range(2):
            lanes = slice(n * WIDE, (n + 1) * WIDE)
            pre = (
                y[64:128, lanes]
                + pltpu.roll(y[0:64, lanes], 1, 1)
                + pltpu.roll(y[128:192, lanes], WIDE - 1, 1)
                + b1
            )
            act = pre / (1.0 + jnp.exp(-pre))
            row = lat_first - 1 + h + n
            if h + n in (0, HID - 1):
                act = jnp.where((row >= 0) & (row < NLAT), act, 0.0)
            hid[(h + n) * 64 : (h + n + 1) * 64, :] = act.astype(jnp.bfloat16)

    w2 = w2_ref[...]
    b2 = b2_ref[...]
    for pair in range(CLAT // 2):
        r = 2 * pair
        x = jnp.concatenate(
            [hid[r * 64 : (r + 3) * 64, :], hid[(r + 1) * 64 : (r + 4) * 64, :]], axis=1
        )
        y = dot(w2, x)
        for n in range(2):
            lanes = slice(n * WIDE, (n + 1) * WIDE)
            total = (
                y[64:128, lanes]
                + pltpu.roll(y[0:64, lanes], 1, 1)
                + pltpu.roll(y[128:192, lanes], WIDE - 1, 1)
            )[:, 0:CLON] + b2
            stage[pl.ds(r + n, CHANNELS, CLAT), :] = total[:, 0:128]
            stage[pl.ds(CHANNELS * CLAT + r + n, CHANNELS, CLAT), :] = total[:, 128:256]
    half = CHANNELS * CLAT
    for n in range(2):
        out_ref[:, :, n * 128 : (n + 1) * 128] = (
            stage[n * half : (n + 1) * half, :].reshape(CHANNELS, CLAT, 128).astype(jnp.bfloat16)
        )


def encode(minus, own, plus, w1, w2, b1, b2, table):
    vmem = pl.BlockSpec(memory_space=pltpu.VMEM)
    bf16, f32 = jnp.bfloat16, jnp.float32
    rows = EXT * SLOT
    partial = pl.pallas_call(
        own_kernel,
        out_shape=[
            jax.ShapeDtypeStruct((rows, INSTR * 128), f32),
            jax.ShapeDtypeStruct((rows, INSTR * 128), f32),
            jax.ShapeDtypeStruct((rows, 128), f32),
        ],
        in_specs=[vmem] * 2,
        out_specs=[vmem] * 3,
        scratch_shapes=[
            pltpu.VMEM((rows, BAND), bf16),
            pltpu.VMEM((INSTR * 128, BAND), bf16),
            pltpu.VMEM((INSTR * 128, BAND), bf16),
            pltpu.VMEM((128, BAND), bf16),
        ],
        compiler_params=pltpu.CompilerParams(vmem_limit_bytes=16 * 1024 * 1024),
        cost_estimate=pl.CostEstimate(flops=2 * rows * BAND * 1152, bytes_accessed=3000000, transcendentals=0),
    )(own, table)
    return pl.pallas_call(
        encode_kernel,
        out_shape=jax.ShapeDtypeStruct((CHANNELS, CLAT, CLON), bf16),
        in_specs=[vmem] * 10,
        out_specs=vmem,
        scratch_shapes=[
            pltpu.VMEM((rows, 2 * BAND), bf16),
            pltpu.VMEM((INSTR * 128, BAND), bf16),
            pltpu.VMEM((INSTR * 128, BAND), bf16),
            pltpu.VMEM((128, 2 * BAND), bf16),
            pltpu.VMEM((rows, INSTR * 128), f32),
            pltpu.VMEM((rows, INSTR * 128), f32),
            pltpu.VMEM((rows, 128), f32),
            pltpu.VMEM((EXT * 128, WIDE), bf16),
            pltpu.VMEM((HID * CHANNELS, WIDE), bf16),
            pltpu.VMEM((2 * CHANNELS * CLAT, 128), f32),
        ],
        compiler_params=pltpu.CompilerParams(vmem_limit_bytes=24 * 1024 * 1024),
    )(minus, plus, table, *partial, w1, b1, w2, b2)


def along(array, shape):
    return lax.broadcast_in_dim(array, shape, (len(shape) - 1,))


def pack(obs_values, obs_lat, obs_lon, instrument):
    shape = (40, ROWS_DEV)
    row = lax.broadcasted_iota(jnp.int32, shape, 0)
    ints = jnp.where(row == 32, along(instrument, shape), 0)
    ints = jnp.where(row == 31, along(obs_lon, shape), ints)
    ints = jnp.where(row == 0, along(obs_lat, shape), ints)
    return jnp.pad(obs_values, ((1, 9), (0, 0))) + ints.astype(jnp.float32)


def pack_small(b_first, b_second, length_scale):
    shape = (8, CHANNELS)
    row = lax.broadcasted_iota(jnp.int32, shape, 0)
    scale = along(jnp.pad(length_scale, (0, CHANNELS - INSTR)), shape)
    small = jnp.where(row == 2, scale, 0.0)
    small = jnp.where(row == 1, along(b_second, shape), small)
    return jnp.where(row == 0, along(b_first, shape), small)


def arrange(w_first, w_second, small):
    bf16, f32 = jnp.bfloat16, jnp.float32
    return pl.pallas_call(
        weights_kernel,
        out_shape=[
            jax.ShapeDtypeStruct((3 * CHANNELS, 3 * 128), bf16),
            jax.ShapeDtypeStruct((3 * CHANNELS, 3 * CHANNELS), bf16),
            jax.ShapeDtypeStruct((CHANNELS, 1), f32),
            jax.ShapeDtypeStruct((CHANNELS, 1), f32),
            jax.ShapeDtypeStruct((2 * INSTR, 128), f32),
        ],
        in_specs=[pl.BlockSpec(memory_space=pltpu.VMEM)] * 3,
        out_specs=[pl.BlockSpec(memory_space=pltpu.VMEM)] * 5,
        compiler_params=pltpu.CompilerParams(vmem_limit_bytes=4 * 1024 * 1024),
        cost_estimate=pl.CostEstimate(flops=20000000, bytes_accessed=1000000, transcendentals=0),
    )(w_first, w_second, small)


def send(array, axis, target):
    peers = lax.axis_size(axis)
    return lax.ppermute(array, axis, [(i, target(i) % peers) for i in range(peers)])


def body(
    obs_values, obs_lat, obs_lon, instrument, length_scale, w_first, b_first, w_second, b_second
):
    rows = pack(obs_values, obs_lat, obs_lon, instrument)
    rows = jnp.concatenate([rows, send(rows, "lat", lambda i: i ^ 1)], axis=1)
    rows, b_first, b_second, length_scale = lax.optimization_barrier(
        (rows, b_first, b_second, length_scale)
    )
    small = pack_small(b_first, b_second, length_scale)
    others = send(rows, "lat", lambda i: i ^ 2)
    rows, others, small, w_first, w_second = lax.optimization_barrier(
        (rows, others, small, w_first, w_second)
    )
    rows = jnp.concatenate([rows, others], axis=1)
    weights = arrange(w_first, w_second, small)
    others = [send(rows, "lat", lambda i, k=k: i + 4 * k) for k in (1, 2, 3)]
    rows, others, weights = lax.optimization_barrier((rows, others, weights))
    rows = jnp.stack([rows] + others)
    minus = send(rows, "lon", lambda i: i + 1)
    plus = send(rows, "lon", lambda i: i - 1)
    return encode(minus, rows, plus, *weights)


def solution(mesh):
    return jax.shard_map(
        body,
        mesh=mesh,
        in_specs=(
            P(None, ("lat", "lon")),
            P(("lat", "lon")),
            P(("lat", "lon")),
            P(("lat", "lon")),
            P(),
            P(),
            P(),
            P(),
            P(),
        ),
        out_specs=P(None, "lat", "lon"),
        check_vma=False,
    )
```

```python
import jax
import jax.numpy as jnp
from jax import lax
from jax.experimental import pallas as pl
from jax.experimental.pallas import tpu as pltpu
from jax.sharding import PartitionSpec as P

CLAT = 16
CLON = 256
INSTR = 4
VALUES = 30
CHANNELS = 64
CIN = 124
SLOT = 32
NLAT = 256
NLON = 4096
ROWS_DEV = 32
PARTS = 4
EXT = CLAT + 4
HID = CLAT + 2
EDGE = 6
BAND = 512
LOG2E = 1.4426950408889634
NT = (((1,), (1,)), ((), ()))
NN = (((1,), (0,)), ((), ()))


def dot(a, b, dims=NN):
    return lax.dot_general(a, b, dims, preferred_element_type=jnp.float32)


def fetch(sources, targets, sems):
    copies = [
        pltpu.make_async_copy(source, target, sems.at[n])
        for n, (source, target) in enumerate(zip(sources, targets, strict=True))
    ]
    for copy in copies:
        copy.start()
    for copy in copies:
        copy.wait()


def weights_kernel(first, second, small, w1, w2, w2_taps, b1, b2, table):
    source = lax.broadcasted_iota(jnp.int32, (CIN, 128), 0)
    slot = lax.broadcasted_iota(jnp.int32, (CIN, 128), 1)
    for k in range(1, INSTR):
        slot = jnp.where(slot == SLOT * k - 1, -1, slot)
    shifted = source
    for k in range(1, INSTR):
        shifted = shifted + jnp.where(source >= k * (VALUES + 1), 1, 0)
    spread = jnp.where(shifted == slot, 1.0, 0.0).astype(jnp.bfloat16)
    for a in range(3):
        for b in range(3):
            rows = slice(b * CHANNELS, (b + 1) * CHANNELS)
            w1[rows, a * 128 : (a + 1) * 128] = dot(first[a, b], spread).astype(jnp.bfloat16)
            w2[rows, a * CHANNELS : (a + 1) * CHANNELS] = second[a, b]
            w2_taps[a, rows, :] = second[a, b]
    up = lax.broadcasted_iota(jnp.int32, (CHANNELS, CHANNELS), 0)
    across = lax.broadcasted_iota(jnp.int32, (CHANNELS, CHANNELS), 1)
    for n, column in enumerate((b1, b2)):
        row = small[n : n + 1, 0:CHANNELS]
        column[...] = jnp.sum(jnp.where(up == across, row, 0.0), axis=1, keepdims=True)
    for k in range(INSTR):
        length = small[2:3, k : k + 1]
        reach = jnp.floor(4.0 * length)
        table[k : k + 1] = jnp.broadcast_to(-LOG2E * (0.5 / (length * length)), (1, 128))
        table[INSTR + k : INSTR + k + 1] = jnp.broadcast_to(reach * reach, (1, 128))


def lon_side():
    return 1 - lax.axis_index("lon") % 2


def build(ref, shift, halves, table, wt, ln, lc):
    lat_first = lax.axis_index("lat") * CLAT
    grid_row = lax.broadcasted_iota(jnp.int32, (24, 128), 0) + (lat_first - 2)
    row_ok = (grid_row >= 0) & (grid_row < NLAT)
    grid_row = grid_row.astype(jnp.float32)
    lane = lax.broadcasted_iota(jnp.int32, (128, 128), 0)
    edge = lax.broadcasted_iota(jnp.int32, (32, 128), 0)
    edge_inst = (edge // EDGE).astype(jnp.float32)
    edge = edge % EDGE
    edge_col = (edge - 2 + jnp.where(edge >= 3, CLON - 2, 0)).astype(jnp.float32)
    which = lax.broadcasted_iota(jnp.int32, (SLOT, 128), 0)
    for block in range(4):
        cols = slice(block * 128, (block + 1) * 128)
        data = ref[block]
        lat = data[0:1]
        lon = data[31:32]
        inst = data[32:33]
        rate = table[0:1]
        reach2 = table[INSTR : INSTR + 1]
        for k in range(1, INSTR):
            rate = jnp.where(inst == float(k), table[k : k + 1], rate)
            reach2 = jnp.where(inst == float(k), table[INSTR + k : INSTR + k + 1], reach2)
        rel = ((lon.astype(jnp.int32) & (CLON - 1)) + shift).astype(jnp.float32)

        def kernel_of(gap):
            gap2 = gap * gap
            return jnp.where(gap2 <= reach2, jnp.exp2(gap2 * rate), 0.0)

        lat_k = jnp.where(row_ok, kernel_of(grid_row - lat), 0.0)
        aug = jnp.where(which == 0, 1.0, jnp.where(which == 31, 0.0, data[0:SLOT]))
        for i in range(EXT):
            wt[i * SLOT : (i + 1) * SLOT, cols] = (lat_k[i : i + 1] * aug).astype(jnp.bfloat16)
        chosen = [jnp.where(inst == float(k), 1.0, 0.0).astype(jnp.bfloat16) for k in range(INSTR)]
        for n, half in enumerate(halves):
            ker = kernel_of((lane + half * 128).astype(jnp.float32) - rel).astype(jnp.bfloat16)
            for k in range(INSTR):
                ln[n, k * 128 : (k + 1) * 128, cols] = ker * chosen[k]
        lc[0:32, cols] = jnp.where(inst == edge_inst, kernel_of(edge_col - rel), 0.0).astype(
            jnp.bfloat16
        )
        lc[32:128, cols] = jnp.zeros((96, 128), jnp.bfloat16)


def features_of(sums):
    density = sums[0:1]
    row = lax.broadcasted_iota(jnp.int32, sums.shape, 0)
    inverse = 1.0 / (1.0 + density)
    return jnp.where(row == 0, jnp.log1p(density), sums * inverse).astype(jnp.bfloat16)


def own_kernel(own_ref, table, s_own, s_edge, wt, ln, lc):
    build(own_ref, 0, (0, 1), table, wt, ln, lc)
    for half in range(2):
        for pair in range(2):
            rows = slice(pair * 256, (pair + 1) * 256)
            s_own[half, :, rows] = dot(wt[...], ln[half, rows, :], NT)
    s_edge[...] = dot(wt[...], lc[...], NT)


def near_kernel(near_ref, table, s_own, s_edge, f_near, edge_out, wt, ln, lc, s_near):
    side = lon_side()
    build(near_ref, (2 * side - 1) * CLON, (side,), table, wt, ln, lc)
    for pair in range(2):
        rows = slice(pair * 256, (pair + 1) * 256)
        s_near[:, rows] = dot(wt[...], ln[0, rows, :], NT)
    edge_out[...] = s_edge[...] + dot(wt[...], lc[...], NT)
    for i in range(EXT):
        rows = slice(i * SLOT, (i + 1) * SLOT)
        for k in range(INSTR):
            lanes = slice(k * 128, (k + 1) * 128)
            f_near[i * 128 + k * SLOT : i * 128 + (k + 1) * SLOT, :] = features_of(
                s_near[rows, lanes] + s_own[side, rows, lanes]
            )


def edge_features(sums):
    lane = lax.broadcasted_iota(jnp.int32, (SLOT, 128), 1)
    parts = [jnp.zeros((SLOT, 128), jnp.float32)] * INSTR
    for i in range(EXT):
        moved = sums[i * SLOT : (i + 1) * SLOT]
        if i > 0:
            moved = pltpu.roll(moved, EDGE * i, 1)
        for k in range(INSTR):
            place = lax.rem(lane - EDGE * (i + k) + 256, 128)
            parts[k] = jnp.where(place < EDGE, moved, parts[k])
    for k in range(1, INSTR):
        parts[k] = pltpu.roll(parts[k], 128 - EDGE * k, 1)
    return jnp.concatenate([features_of(part) for part in parts], axis=0)


def edge_terms(products):
    left = products[0][0:CHANNELS]
    right = products[0][2 * CHANNELS : 3 * CHANNELS]
    for a in (1, 2):
        left += pltpu.roll(products[a][0:CHANNELS], 128 - EDGE * a, 1)
        right += pltpu.roll(products[a][2 * CHANNELS : 3 * CHANNELS], 128 - EDGE * a, 1)
    lane = lax.broadcasted_iota(jnp.int32, left.shape, 1)
    return jnp.where(lax.rem(lane, EDGE) == 1, left, pltpu.roll(right, 128 - 4, 1))


def row_total(y, terms, row, bias):
    left = pltpu.roll(y[0:CHANNELS], 1, 1)
    right = pltpu.roll(y[2 * CHANNELS : 3 * CHANNELS], CLON - 1, 1)
    here = pltpu.roll(terms, 128 - (EDGE * row + 1), 1)
    lane = lax.broadcasted_iota(jnp.int32, here.shape, 1)
    middle = y[CHANNELS : 2 * CHANNELS] + bias
    return (
        middle[:, 0:128] + jnp.where(lane == 0, here, left[:, 0:128]) + right[:, 0:128],
        middle[:, 128:256] + left[:, 128:256] + jnp.where(lane == 127, here, right[:, 128:256]),
    )


def silu(x):
    return x / (1.0 + jnp.exp(-x))


def encode_kernel(
    far_ref, table, s_own, s_edge, f_near, w1_ref, w2_ref, w2_taps, b1_ref, b2_ref,
    out_ref, wt, ln, lc, s_far, feat, hid, stage, result, sems,
):
    lat_first = lax.axis_index("lat") * CLAT
    near_side = lon_side()
    side = 1 - near_side
    build(far_ref, (2 * side - 1) * CLON, (side,), table, wt, ln, lc)
    edge_sums = s_edge[...] + dot(wt[...], lc[...], NT)
    for pair in range(2):
        rows = slice(pair * 256, (pair + 1) * 256)
        s_far[:, rows] = dot(wt[...], ln[0, rows, :], NT)
    for i in range(EXT):
        rows = slice(i * SLOT, (i + 1) * SLOT)
        for k in range(INSTR):
            lanes = slice(k * 128, (k + 1) * 128)
            slot = slice(i * 128 + k * SLOT, i * 128 + (k + 1) * SLOT)
            far = features_of(s_far[rows, lanes] + s_own[side, rows, lanes])
            near = f_near[slot, :]
            feat[slot, 0:128] = jnp.where(near_side == 0, near, far)
            feat[slot, 128:256] = jnp.where(near_side == 0, far, near)

    w1 = w1_ref[...]
    b1 = b1_ref[...]
    edge_feat = edge_features(edge_sums)
    products = [dot(w1[:, a * 128 : (a + 1) * 128], edge_feat) for a in range(3)]
    terms = edge_terms(products)
    pre = b1
    for a in range(3):
        for b in range(3):
            part = products[a][b * CHANNELS : (b + 1) * CHANNELS]
            shift = (EDGE * a + b - 1) % 128
            pre = pre + (part if shift == 0 else pltpu.roll(part, 128 - shift, 1))
    lane_row = lax.broadcasted_iota(jnp.int32, (CHANNELS, 128), 1) // EDGE + lat_first - 1
    inside = (lane_row >= 0) & (lane_row < NLAT)
    edge_hid = jnp.where(inside, silu(pre), 0.0).astype(jnp.bfloat16)
    for h in range(HID):
        y = dot(w1, feat[h * 128 : (h + 3) * 128, :])
        row = lat_first - 1 + h
        for n, half in enumerate(row_total(y, terms, h, b1)):
            act = silu(half)
            if h in (0, HID - 1):
                act = jnp.where((row >= 0) & (row < NLAT), act, 0.0)
            hid[h * CHANNELS : (h + 1) * CHANNELS, n * 128 : (n + 1) * 128] = act.astype(jnp.bfloat16)

    w2 = w2_ref[...]
    b2 = b2_ref[...]
    terms = edge_terms([dot(w2_taps[a], edge_hid) for a in range(3)])
    size = CHANNELS * CLAT
    for r in range(CLAT):
        y = dot(w2, hid[r * CHANNELS : (r + 3) * CHANNELS, :])
        for n, half in enumerate(row_total(y, terms, r, b2)):
            stage[pl.ds(n * size + r, CHANNELS, CLAT), :] = half

    copies = []
    step = CHANNELS // PARTS
    for part in range(PARTS):
        channels = slice(part * step, (part + 1) * step)
        for n in range(2):
            result[channels, :, n * 128 : (n + 1) * 128] = (
                stage[n * size + part * step * CLAT : n * size + (part + 1) * step * CLAT, :]
                .reshape(step, CLAT, 128)
                .astype(jnp.bfloat16)
            )
        copies.append(
            pltpu.make_async_copy(result.at[channels], out_ref.at[channels], sems.at[part])
        )
        copies[-1].start()
    for copy in copies:
        copy.wait()


def encode(near, own, far, w1, w2, w2_taps, b1, b2, table):
    vmem = pl.BlockSpec(memory_space=pltpu.VMEM)
    bf16, f32 = jnp.bfloat16, jnp.float32
    rows = EXT * SLOT
    s_own, s_edge = pl.pallas_call(
        own_kernel,
        out_shape=[
            jax.ShapeDtypeStruct((2, rows, INSTR * 128), f32),
            jax.ShapeDtypeStruct((rows, 128), f32),
        ],
        in_specs=[vmem] * 2,
        out_specs=[vmem] * 2,
        scratch_shapes=[
            pltpu.VMEM((rows, BAND), bf16),
            pltpu.VMEM((2, INSTR * 128, BAND), bf16),
            pltpu.VMEM((128, BAND), bf16),
        ],
        compiler_params=pltpu.CompilerParams(vmem_limit_bytes=16 * 1024 * 1024),
        cost_estimate=pl.CostEstimate(flops=2 * rows * BAND * 1152, bytes_accessed=3000000, transcendentals=0),
    )(own, table)
    f_near, s_edge = pl.pallas_call(
        near_kernel,
        out_shape=[
            jax.ShapeDtypeStruct((EXT * 128, 128), bf16),
            jax.ShapeDtypeStruct((rows, 128), f32),
        ],
        in_specs=[vmem] * 4,
        out_specs=[vmem] * 2,
        scratch_shapes=[
            pltpu.VMEM((rows, BAND), bf16),
            pltpu.VMEM((1, INSTR * 128, BAND), bf16),
            pltpu.VMEM((128, BAND), bf16),
            pltpu.VMEM((rows, INSTR * 128), f32),
        ],
        compiler_params=pltpu.CompilerParams(vmem_limit_bytes=16 * 1024 * 1024),
        cost_estimate=pl.CostEstimate(flops=2 * rows * BAND * 640, bytes_accessed=3000000, transcendentals=0),
    )(near, table, s_own, s_edge)
    return pl.pallas_call(
        encode_kernel,
        out_shape=jax.ShapeDtypeStruct((CHANNELS, CLAT, CLON), bf16),
        in_specs=[vmem] * 10,
        out_specs=pl.BlockSpec(memory_space=pl.ANY),
        scratch_shapes=[
            pltpu.VMEM((rows, BAND), bf16),
            pltpu.VMEM((1, INSTR * 128, BAND), bf16),
            pltpu.VMEM((128, BAND), bf16),
            pltpu.VMEM((rows, INSTR * 128), f32),
            pltpu.VMEM((EXT * 128, CLON), bf16),
            pltpu.VMEM((HID * CHANNELS, CLON), bf16),
            pltpu.VMEM((2 * CHANNELS * CLAT, 128), f32),
            pltpu.VMEM((CHANNELS, CLAT, CLON), bf16),
            pltpu.SemaphoreType.DMA((PARTS,)),
        ],
        compiler_params=pltpu.CompilerParams(vmem_limit_bytes=24 * 1024 * 1024),
    )(far, table, s_own, s_edge, f_near, w1, w2, w2_taps, b1, b2)


def along(array, shape):
    return lax.broadcast_in_dim(array, shape, (len(shape) - 1,))


def pack(obs_values, obs_lat, obs_lon, instrument):
    shape = (40, ROWS_DEV)
    row = lax.broadcasted_iota(jnp.int32, shape, 0)
    ints = jnp.where(row == 32, along(instrument, shape), 0)
    ints = jnp.where(row == 31, along(obs_lon, shape), ints)
    ints = jnp.where(row == 0, along(obs_lat, shape), ints)
    return jnp.pad(obs_values, ((1, 9), (0, 0))) + ints.astype(jnp.float32)


def pack_small(b_first, b_second, length_scale):
    shape = (8, CHANNELS)
    row = lax.broadcasted_iota(jnp.int32, shape, 0)
    scale = along(jnp.pad(length_scale, (0, CHANNELS - INSTR)), shape)
    small = jnp.where(row == 2, scale, 0.0)
    small = jnp.where(row == 1, along(b_second, shape), small)
    return jnp.where(row == 0, along(b_first, shape), small)


def arrange(w_first, w_second, small):
    bf16, f32 = jnp.bfloat16, jnp.float32
    return pl.pallas_call(
        weights_kernel,
        out_shape=[
            jax.ShapeDtypeStruct((3 * CHANNELS, 3 * 128), bf16),
            jax.ShapeDtypeStruct((3 * CHANNELS, 3 * CHANNELS), bf16),
            jax.ShapeDtypeStruct((3, 3 * CHANNELS, CHANNELS), bf16),
            jax.ShapeDtypeStruct((CHANNELS, 1), f32),
            jax.ShapeDtypeStruct((CHANNELS, 1), f32),
            jax.ShapeDtypeStruct((2 * INSTR, 128), f32),
        ],
        in_specs=[pl.BlockSpec(memory_space=pltpu.VMEM)] * 3,
        out_specs=[pl.BlockSpec(memory_space=pltpu.VMEM)] * 6,
        compiler_params=pltpu.CompilerParams(vmem_limit_bytes=4 * 1024 * 1024),
        cost_estimate=pl.CostEstimate(flops=20000000, bytes_accessed=1000000, transcendentals=0),
    )(w_first, w_second, small)


def send(array, axis, target):
    peers = lax.axis_size(axis)
    return lax.ppermute(array, axis, [(i, target(i) % peers) for i in range(peers)])


def body(
    obs_values, obs_lat, obs_lon, instrument, length_scale, w_first, b_first, w_second, b_second
):
    rows = pack(obs_values, obs_lat, obs_lon, instrument)
    rows = jnp.concatenate([rows, send(rows, "lat", lambda i: i ^ 1)], axis=1)
    rows, b_first, b_second, length_scale = lax.optimization_barrier(
        (rows, b_first, b_second, length_scale)
    )
    small = pack_small(b_first, b_second, length_scale)
    others = send(rows, "lat", lambda i: i ^ 2)
    rows, others, small, w_first, w_second = lax.optimization_barrier(
        (rows, others, small, w_first, w_second)
    )
    rows = jnp.concatenate([rows, others], axis=1)
    weights = arrange(w_first, w_second, small)
    others = [send(rows, "lat", lambda i, k=k: i + 4 * k) for k in (3, 2, 1)]
    rows, others, weights = lax.optimization_barrier((rows, others, weights))
    rows = jnp.stack([rows] + others)
    near = send(rows, "lon", lambda i: i ^ 1)
    far = send(rows, "lon", lambda i: ((i + 1) ^ 1) - 1)
    return encode(near, rows, far, *weights)


def solution(mesh):
    return jax.shard_map(
        body,
        mesh=mesh,
        in_specs=(
            P(None, ("lat", "lon")),
            P(("lat", "lon")),
            P(("lat", "lon")),
            P(("lat", "lon")),
            P(),
            P(),
            P(),
            P(),
            P(),
        ),
        out_specs=P(None, "lat", "lon"),
        check_vma=False,
    )
```

```python
import jax
import jax.numpy as jnp
from jax import lax
from jax.experimental import pallas as pl
from jax.experimental.pallas import tpu as pltpu
from jax.sharding import PartitionSpec as P

CLAT = 16
CLON = 256
INSTR = 4
VALUES = 30
CHANNELS = 64
CIN = 124
SLOT = 32
NLAT = 256
NLON = 4096
ROWS_DEV = 32
PARTS = 4
EXT = CLAT + 4
HID = CLAT + 2
EDGE = 6
BAND = 512
LOG2E = 1.4426950408889634
NT = (((1,), (1,)), ((), ()))
NN = (((1,), (0,)), ((), ()))


def dot(a, b, dims=NN):
    return lax.dot_general(a, b, dims, preferred_element_type=jnp.float32)


def fetch(sources, targets, sems):
    copies = [
        pltpu.make_async_copy(source, target, sems.at[n])
        for n, (source, target) in enumerate(zip(sources, targets, strict=True))
    ]
    for copy in copies:
        copy.start()
    for copy in copies:
        copy.wait()


def weights_kernel(both, small, w1, w2, w2_taps, b1, b2, table):
    source = lax.broadcasted_iota(jnp.int32, (CIN, 128), 0)
    slot = lax.broadcasted_iota(jnp.int32, (CIN, 128), 1)
    shifted = source
    for k in range(1, INSTR):
        slot = jnp.where(slot == SLOT * k - 1, -1, slot)
        shifted = shifted + jnp.where(source >= k * (VALUES + 1), 1, 0)
    spread = jnp.where(shifted == slot, 1.0, 0.0).astype(jnp.bfloat16)
    for a in range(3):
        for b in range(3):
            rows = slice(b * CHANNELS, (b + 1) * CHANNELS)
            first = both[a, b, 0:CHANNELS, :]
            second = both[a, b, CHANNELS : 2 * CHANNELS, 0:CHANNELS]
            w1[rows, a * 128 : (a + 1) * 128] = dot(first, spread).astype(jnp.bfloat16)
            w2[rows, a * CHANNELS : (a + 1) * CHANNELS] = second
            w2_taps[a, rows, :] = second
    up = lax.broadcasted_iota(jnp.int32, (CHANNELS, CHANNELS), 0)
    across = lax.broadcasted_iota(jnp.int32, (CHANNELS, CHANNELS), 1)
    for n, column in enumerate((b1, b2)):
        row = small[n : n + 1, 0:CHANNELS]
        column[...] = jnp.sum(jnp.where(up == across, row, 0.0), axis=1, keepdims=True)
    for k in range(INSTR):
        length = small[2:3, k : k + 1]
        reach = jnp.floor(4.0 * length)
        table[k : k + 1] = jnp.broadcast_to(-LOG2E * (0.5 / (length * length)), (1, 128))
        table[INSTR + k : INSTR + k + 1] = jnp.broadcast_to(reach * reach, (1, 128))


def lon_side():
    return 1 - lax.axis_index("lon") % 2


def build(ref, shift, halves, table, wt, ln, lc):
    lat_first = lax.axis_index("lat") * CLAT
    grid_row = lax.broadcasted_iota(jnp.int32, (24, 128), 0) + (lat_first - 2)
    row_ok = (grid_row >= 0) & (grid_row < NLAT)
    grid_row = grid_row.astype(jnp.float32)
    lane = lax.broadcasted_iota(jnp.int32, (128, 128), 0)
    edge = lax.broadcasted_iota(jnp.int32, (32, 128), 0)
    edge_inst = (edge // EDGE).astype(jnp.float32)
    edge = edge % EDGE
    edge_col = (edge - 2 + jnp.where(edge >= 3, CLON - 2, 0)).astype(jnp.float32)
    which = lax.broadcasted_iota(jnp.int32, (SLOT, 128), 0)
    for block in range(4):
        cols = slice(block * 128, (block + 1) * 128)
        data = ref[block]
        code = data[0:1].astype(jnp.int32)
        lat = (code // INSTR).astype(jnp.float32)
        inst = (code % INSTR).astype(jnp.float32)
        lon = data[31:32]
        rate = table[0:1]
        reach2 = table[INSTR : INSTR + 1]
        for k in range(1, INSTR):
            rate = jnp.where(inst == float(k), table[k : k + 1], rate)
            reach2 = jnp.where(inst == float(k), table[INSTR + k : INSTR + k + 1], reach2)
        rel = ((lon.astype(jnp.int32) & (CLON - 1)) + shift).astype(jnp.float32)

        def kernel_of(gap):
            gap2 = gap * gap
            return jnp.where(gap2 <= reach2, jnp.exp2(gap2 * rate), 0.0)

        lat_k = jnp.where(row_ok, kernel_of(grid_row - lat), 0.0)
        aug = jnp.where(which == 0, 1.0, jnp.where(which == 31, 0.0, data[0:SLOT]))
        for i in range(EXT):
            wt[i * SLOT : (i + 1) * SLOT, cols] = (lat_k[i : i + 1] * aug).astype(jnp.bfloat16)
        chosen = [jnp.where(inst == float(k), 1.0, 0.0).astype(jnp.bfloat16) for k in range(INSTR)]
        for n, half in enumerate(halves):
            ker = kernel_of((lane + half * 128).astype(jnp.float32) - rel).astype(jnp.bfloat16)
            for k in range(INSTR):
                ln[n, k * 128 : (k + 1) * 128, cols] = ker * chosen[k]
        lc[0:32, cols] = jnp.where(inst == edge_inst, kernel_of(edge_col - rel), 0.0).astype(
            jnp.bfloat16
        )
        lc[32:128, cols] = jnp.zeros((96, 128), jnp.bfloat16)


def features_of(sums):
    density = sums[0:1]
    row = lax.broadcasted_iota(jnp.int32, sums.shape, 0)
    inverse = 1.0 / (1.0 + density)
    return jnp.where(row == 0, jnp.log1p(density), sums * inverse).astype(jnp.bfloat16)


def own_kernel(own_ref, table, s_own, s_edge, wt, ln, lc):
    build(own_ref, 0, (0, 1), table, wt, ln, lc)
    for half in range(2):
        for pair in range(2):
            rows = slice(pair * 256, (pair + 1) * 256)
            s_own[half, :, rows] = dot(wt[...], ln[half, rows, :], NT)
    s_edge[...] = dot(wt[...], lc[...], NT)


def near_kernel(near_ref, table, s_own, s_edge, f_near, edge_out, wt, ln, lc, s_near):
    side = lon_side()
    build(near_ref, (2 * side - 1) * CLON, (side,), table, wt, ln, lc)
    for pair in range(2):
        rows = slice(pair * 256, (pair + 1) * 256)
        s_near[:, rows] = dot(wt[...], ln[0, rows, :], NT)
    edge_out[...] = s_edge[...] + dot(wt[...], lc[...], NT)
    for i in range(EXT):
        rows = slice(i * SLOT, (i + 1) * SLOT)
        for k in range(INSTR):
            lanes = slice(k * 128, (k + 1) * 128)
            f_near[i * 128 + k * SLOT : i * 128 + (k + 1) * SLOT, :] = features_of(
                s_near[rows, lanes] + s_own[side, rows, lanes]
            )


def edge_features(sums):
    lane = lax.broadcasted_iota(jnp.int32, (SLOT, 128), 1)
    parts = [jnp.zeros((SLOT, 128), jnp.float32)] * INSTR
    for i in range(EXT):
        moved = sums[i * SLOT : (i + 1) * SLOT]
        if i > 0:
            moved = pltpu.roll(moved, EDGE * i, 1)
        for k in range(INSTR):
            place = lax.rem(lane - EDGE * (i + k) + 256, 128)
            parts[k] = jnp.where(place < EDGE, moved, parts[k])
    for k in range(1, INSTR):
        parts[k] = pltpu.roll(parts[k], 128 - EDGE * k, 1)
    return jnp.concatenate([features_of(part) for part in parts], axis=0)


def edge_terms(products):
    left = products[0][0:CHANNELS]
    right = products[0][2 * CHANNELS : 3 * CHANNELS]
    for a in (1, 2):
        left += pltpu.roll(products[a][0:CHANNELS], 128 - EDGE * a, 1)
        right += pltpu.roll(products[a][2 * CHANNELS : 3 * CHANNELS], 128 - EDGE * a, 1)
    lane = lax.broadcasted_iota(jnp.int32, left.shape, 1)
    return jnp.where(lax.rem(lane, EDGE) == 1, left, pltpu.roll(right, 128 - 4, 1))


def row_total(y, terms, row, bias):
    left = pltpu.roll(y[0:CHANNELS], 1, 1)
    right = pltpu.roll(y[2 * CHANNELS : 3 * CHANNELS], CLON - 1, 1)
    here = pltpu.roll(terms, 128 - (EDGE * row + 1), 1)
    lane = lax.broadcasted_iota(jnp.int32, here.shape, 1)
    middle = y[CHANNELS : 2 * CHANNELS] + bias
    return (
        middle[:, 0:128] + jnp.where(lane == 0, here, left[:, 0:128]) + right[:, 0:128],
        middle[:, 128:256] + left[:, 128:256] + jnp.where(lane == 127, here, right[:, 128:256]),
    )


def silu(x):
    return x / (1.0 + jnp.exp(-x))


def encode_kernel(
    far_ref, table, s_own, s_edge, f_near, w1_ref, w2_ref, w2_taps, b1_ref, b2_ref,
    out_ref, wt, ln, lc, s_far, feat, hid, stage, result, sems,
):
    lat_first = lax.axis_index("lat") * CLAT
    near_side = lon_side()
    side = 1 - near_side
    build(far_ref, (2 * side - 1) * CLON, (side,), table, wt, ln, lc)
    edge_sums = s_edge[...] + dot(wt[...], lc[...], NT)
    for pair in range(2):
        rows = slice(pair * 256, (pair + 1) * 256)
        s_far[:, rows] = dot(wt[...], ln[0, rows, :], NT)
    for i in range(EXT):
        rows = slice(i * SLOT, (i + 1) * SLOT)
        for k in range(INSTR):
            lanes = slice(k * 128, (k + 1) * 128)
            slot = slice(i * 128 + k * SLOT, i * 128 + (k + 1) * SLOT)
            far = features_of(s_far[rows, lanes] + s_own[side, rows, lanes])
            near = f_near[slot, :]
            feat[slot, 0:128] = jnp.where(near_side == 0, near, far)
            feat[slot, 128:256] = jnp.where(near_side == 0, far, near)

    w1 = w1_ref[...]
    b1 = b1_ref[...]
    edge_feat = edge_features(edge_sums)
    products = [dot(w1[:, a * 128 : (a + 1) * 128], edge_feat) for a in range(3)]
    terms = edge_terms(products)
    pre = b1
    for a in range(3):
        for b in range(3):
            part = products[a][b * CHANNELS : (b + 1) * CHANNELS]
            shift = (EDGE * a + b - 1) % 128
            pre = pre + (part if shift == 0 else pltpu.roll(part, 128 - shift, 1))
    lane_row = lax.broadcasted_iota(jnp.int32, (CHANNELS, 128), 1) // EDGE + lat_first - 1
    inside = (lane_row >= 0) & (lane_row < NLAT)
    edge_hid = jnp.where(inside, silu(pre), 0.0).astype(jnp.bfloat16)
    for h in range(HID):
        y = dot(w1, feat[h * 128 : (h + 3) * 128, :])
        row = lat_first - 1 + h
        for n, half in enumerate(row_total(y, terms, h, b1)):
            act = silu(half)
            if h in (0, HID - 1):
                act = jnp.where((row >= 0) & (row < NLAT), act, 0.0)
            hid[h * CHANNELS : (h + 1) * CHANNELS, n * 128 : (n + 1) * 128] = act.astype(jnp.bfloat16)

    w2 = w2_ref[...]
    b2 = b2_ref[...]
    terms = edge_terms([dot(w2_taps[a], edge_hid) for a in range(3)])
    size = CHANNELS * CLAT
    for r in range(CLAT):
        y = dot(w2, hid[r * CHANNELS : (r + 3) * CHANNELS, :])
        for n, half in enumerate(row_total(y, terms, r, b2)):
            stage[pl.ds(n * size + r, CHANNELS, CLAT), :] = half

    copies = []
    step = CHANNELS // PARTS
    for part in range(PARTS):
        channels = slice(part * step, (part + 1) * step)
        for n in range(2):
            result[channels, :, n * 128 : (n + 1) * 128] = (
                stage[n * size + part * step * CLAT : n * size + (part + 1) * step * CLAT, :]
                .reshape(step, CLAT, 128)
                .astype(jnp.bfloat16)
            )
        copies.append(
            pltpu.make_async_copy(result.at[channels], out_ref.at[channels], sems.at[part])
        )
        copies[-1].start()
    for copy in copies:
        copy.wait()


def encode(near, own, far, w1, w2, w2_taps, b1, b2, table):
    vmem = pl.BlockSpec(memory_space=pltpu.VMEM)
    bf16, f32 = jnp.bfloat16, jnp.float32
    rows = EXT * SLOT
    s_own, s_edge = pl.pallas_call(
        own_kernel,
        out_shape=[
            jax.ShapeDtypeStruct((2, rows, INSTR * 128), f32),
            jax.ShapeDtypeStruct((rows, 128), f32),
        ],
        in_specs=[vmem] * 2,
        out_specs=[vmem] * 2,
        scratch_shapes=[
            pltpu.VMEM((rows, BAND), bf16),
            pltpu.VMEM((2, INSTR * 128, BAND), bf16),
            pltpu.VMEM((128, BAND), bf16),
        ],
        compiler_params=pltpu.CompilerParams(vmem_limit_bytes=16 * 1024 * 1024),
        cost_estimate=pl.CostEstimate(flops=2 * rows * BAND * 1152, bytes_accessed=3000000, transcendentals=0),
    )(own, table)
    f_near, s_edge = pl.pallas_call(
        near_kernel,
        out_shape=[
            jax.ShapeDtypeStruct((EXT * 128, 128), bf16),
            jax.ShapeDtypeStruct((rows, 128), f32),
        ],
        in_specs=[vmem] * 4,
        out_specs=[vmem] * 2,
        scratch_shapes=[
            pltpu.VMEM((rows, BAND), bf16),
            pltpu.VMEM((1, INSTR * 128, BAND), bf16),
            pltpu.VMEM((128, BAND), bf16),
            pltpu.VMEM((rows, INSTR * 128), f32),
        ],
        compiler_params=pltpu.CompilerParams(vmem_limit_bytes=16 * 1024 * 1024),
        cost_estimate=pl.CostEstimate(flops=2 * rows * BAND * 640, bytes_accessed=3000000, transcendentals=0),
    )(near, table, s_own, s_edge)
    return pl.pallas_call(
        encode_kernel,
        out_shape=jax.ShapeDtypeStruct((CHANNELS, CLAT, CLON), bf16),
        in_specs=[vmem] * 10,
        out_specs=pl.BlockSpec(memory_space=pl.ANY),
        scratch_shapes=[
            pltpu.VMEM((rows, BAND), bf16),
            pltpu.VMEM((1, INSTR * 128, BAND), bf16),
            pltpu.VMEM((128, BAND), bf16),
            pltpu.VMEM((rows, INSTR * 128), f32),
            pltpu.VMEM((EXT * 128, CLON), bf16),
            pltpu.VMEM((HID * CHANNELS, CLON), bf16),
            pltpu.VMEM((2 * CHANNELS * CLAT, 128), f32),
            pltpu.VMEM((CHANNELS, CLAT, CLON), bf16),
            pltpu.SemaphoreType.DMA((PARTS,)),
        ],
        compiler_params=pltpu.CompilerParams(vmem_limit_bytes=24 * 1024 * 1024),
    )(far, table, s_own, s_edge, f_near, w1, w2, w2_taps, b1, b2)


def along(array, shape):
    return lax.broadcast_in_dim(array, shape, (len(shape) - 1,))


def pack(obs_values, obs_lat, obs_lon, instrument):
    shape = (SLOT, ROWS_DEV)
    row = lax.broadcasted_iota(jnp.int32, shape, 0)
    high = jnp.where(row == 0, along(obs_lat, shape), 0)
    ints = jnp.where(row == 31, along(obs_lon, shape), 0)
    ints = jnp.where(row == 0, along(instrument, shape), ints)
    return jnp.pad(obs_values, ((1, 1), (0, 0))) + (high * INSTR + ints).astype(jnp.float32)


def pack_small(b_first, b_second, scale):
    shape = (8, CHANNELS)
    row = lax.broadcasted_iota(jnp.int32, shape, 0)
    small = jnp.where(row == 2, along(scale, shape), 0.0)
    small = jnp.where(row == 1, along(b_second, shape), small)
    return jnp.where(row == 0, along(b_first, shape), small)


def arrange(w_first, w_second, small):
    bf16, f32 = jnp.bfloat16, jnp.float32
    wide = jnp.pad(w_second, ((0, 0), (0, 0), (CHANNELS, 0), (0, CIN - CHANNELS)))
    both = jnp.pad(w_first, ((0, 0), (0, 0), (0, CHANNELS), (0, 0))) + wide
    return pl.pallas_call(
        weights_kernel,
        out_shape=[
            jax.ShapeDtypeStruct((3 * CHANNELS, 3 * 128), bf16),
            jax.ShapeDtypeStruct((3 * CHANNELS, 3 * CHANNELS), bf16),
            jax.ShapeDtypeStruct((3, 3 * CHANNELS, CHANNELS), bf16),
            jax.ShapeDtypeStruct((CHANNELS, 1), f32),
            jax.ShapeDtypeStruct((CHANNELS, 1), f32),
            jax.ShapeDtypeStruct((2 * INSTR, 128), f32),
        ],
        in_specs=[pl.BlockSpec(memory_space=pltpu.VMEM)] * 2,
        out_specs=[pl.BlockSpec(memory_space=pltpu.VMEM)] * 6,
        compiler_params=pltpu.CompilerParams(vmem_limit_bytes=4 * 1024 * 1024),
        cost_estimate=pl.CostEstimate(flops=20000000, bytes_accessed=1000000, transcendentals=0),
    )(both, small)


def send(array, axis, target):
    peers = lax.axis_size(axis)
    return lax.ppermute(array, axis, [(i, target(i) % peers) for i in range(peers)])


def body(
    obs_values, obs_lat, obs_lon, instrument, length_scale, w_first, b_first, w_second, b_second
):
    rows = pack(obs_values, obs_lat, obs_lon, instrument)
    rows, length_scale = lax.optimization_barrier((rows, length_scale))
    scale = jnp.pad(length_scale, (0, CHANNELS - INSTR))
    others = send(rows, "lat", lambda i: i ^ 1)
    rows, others, scale, b_first, b_second, w_first, w_second = lax.optimization_barrier(
        (rows, others, scale, b_first, b_second, w_first, w_second)
    )
    rows = jnp.concatenate([rows, others], axis=1)
    rows, b_first, b_second, w_first, w_second = lax.optimization_barrier(
        (rows, b_first, b_second, w_first, w_second)
    )
    weights = arrange(w_first, w_second, pack_small(b_first, b_second, scale))
    others = send(rows, "lat", lambda i: i ^ 2)
    rows, others, weights = lax.optimization_barrier((rows, others, weights))
    rows = jnp.concatenate([rows, others], axis=1)
    across = send(rows, "lat", lambda i: i ^ 8)
    beside = send(rows, "lat", lambda i: i + 4 if i % 2 == 0 else i - 4)
    others = [across, send(beside, "lat", lambda i: i ^ 1), beside]
    rows = jnp.stack([rows] + others)
    near = send(rows, "lon", lambda i: i ^ 1)
    far = send(rows, "lon", lambda i: ((i + 1) ^ 1) - 1)
    return encode(near, rows, far, *weights)


def solution(mesh):
    return jax.shard_map(
        body,
        mesh=mesh,
        in_specs=(
            P(None, ("lat", "lon")),
            P(("lat", "lon")),
            P(("lat", "lon")),
            P(("lat", "lon")),
            P(),
            P(),
            P(),
            P(),
            P(),
        ),
        out_specs=P(None, "lat", "lon"),
        check_vma=False,
    )
```

```python
import jax
import jax.numpy as jnp
from jax import lax
from jax.experimental import pallas as pl
from jax.experimental.pallas import tpu as pltpu
from jax.sharding import PartitionSpec as P

CLAT = 16
CLON = 256
INSTR = 4
VALUES = 30
CHANNELS = 64
CIN = 124
SLOT = 32
NLAT = 256
NLON = 4096
ROWS_DEV = 32
STEP = 24
PARTS = 4
EXT = CLAT + 4
HID = CLAT + 2
EDGE = 6
BAND = 512
LOG2E = 1.4426950408889634
NT = (((1,), (1,)), ((), ()))
NN = (((1,), (0,)), ((), ()))


def dot(a, b, dims=NN):
    return lax.dot_general(a, b, dims, preferred_element_type=jnp.float32)


def fetch(sources, targets, sems):
    copies = [
        pltpu.make_async_copy(source, target, sems.at[n])
        for n, (source, target) in enumerate(zip(sources, targets, strict=True))
    ]
    for copy in copies:
        copy.start()
    for copy in copies:
        copy.wait()


def weights_kernel(both, small, w1, w2, w2_taps, b1, b2, table):
    source = lax.broadcasted_iota(jnp.int32, (CIN, 128), 0)
    slot = lax.broadcasted_iota(jnp.int32, (CIN, 128), 1)
    shifted = source
    for k in range(1, INSTR):
        slot = jnp.where(slot == SLOT * k - 1, -1, slot)
        shifted = shifted + jnp.where(source >= k * (VALUES + 1), 1, 0)
    spread = jnp.where(shifted == slot, 1.0, 0.0).astype(jnp.bfloat16)
    for a in range(3):
        for b in range(3):
            rows = slice(b * CHANNELS, (b + 1) * CHANNELS)
            first = both[a, b, 0:CHANNELS, :]
            second = both[a, b, CHANNELS : 2 * CHANNELS, 0:CHANNELS]
            w1[rows, a * 128 : (a + 1) * 128] = dot(first, spread).astype(jnp.bfloat16)
            w2[rows, a * CHANNELS : (a + 1) * CHANNELS] = second
            w2_taps[a, rows, :] = second
    up = lax.broadcasted_iota(jnp.int32, (CHANNELS, CHANNELS), 0)
    across = lax.broadcasted_iota(jnp.int32, (CHANNELS, CHANNELS), 1)
    for n, column in enumerate((b1, b2)):
        row = small[n : n + 1, 0:CHANNELS]
        column[...] = jnp.sum(jnp.where(up == across, row, 0.0), axis=1, keepdims=True)
    for k in range(INSTR):
        length = small[2:3, k : k + 1]
        reach = jnp.floor(4.0 * length)
        table[k : k + 1] = jnp.broadcast_to(-LOG2E * (0.5 / (length * length)), (1, 128))
        table[INSTR + k : INSTR + k + 1] = jnp.broadcast_to(reach * reach, (1, 128))


def lon_side():
    return 1 - lax.axis_index("lon") % 2


def build(ref, shift, halves, table, wt, ln, lc):
    lat_first = lax.axis_index("lat") * CLAT
    grid_row = lax.broadcasted_iota(jnp.int32, (24, 128), 0) + (lat_first - 2)
    row_ok = (grid_row >= 0) & (grid_row < NLAT)
    grid_row = grid_row.astype(jnp.float32)
    lane = lax.broadcasted_iota(jnp.int32, (128, 128), 0)
    edge = lax.broadcasted_iota(jnp.int32, (32, 128), 0)
    edge_inst = (edge // EDGE).astype(jnp.float32)
    edge = edge % EDGE
    edge_col = (edge - 2 + jnp.where(edge >= 3, CLON - 2, 0)).astype(jnp.float32)
    which = lax.broadcasted_iota(jnp.int32, (SLOT, 128), 0)
    for block in range(4):
        cols = slice(block * 128, (block + 1) * 128)
        data = ref[block]
        code = data[0:1].astype(jnp.int32)
        lat = (code // INSTR).astype(jnp.float32)
        inst = (code % INSTR).astype(jnp.float32)
        lon = data[31:32]
        rate = table[0:1]
        reach2 = table[INSTR : INSTR + 1]
        for k in range(1, INSTR):
            rate = jnp.where(inst == float(k), table[k : k + 1], rate)
            reach2 = jnp.where(inst == float(k), table[INSTR + k : INSTR + k + 1], reach2)
        rel = ((lon.astype(jnp.int32) & (CLON - 1)) + shift).astype(jnp.float32)

        def kernel_of(gap):
            gap2 = gap * gap
            return jnp.where(gap2 <= reach2, jnp.exp2(gap2 * rate), 0.0)

        lat_k = jnp.where(row_ok, kernel_of(grid_row - lat), 0.0)
        aug = jnp.where(which == 0, 1.0, jnp.where(which == 31, 0.0, data[0:SLOT]))
        for i in range(EXT):
            wt[i * SLOT : (i + 1) * SLOT, cols] = (lat_k[i : i + 1] * aug).astype(jnp.bfloat16)
        chosen = [jnp.where(inst == float(k), 1.0, 0.0).astype(jnp.bfloat16) for k in range(INSTR)]
        for n, half in enumerate(halves):
            ker = kernel_of((lane + half * 128).astype(jnp.float32) - rel).astype(jnp.bfloat16)
            for k in range(INSTR):
                ln[n, k * 128 : (k + 1) * 128, cols] = ker * chosen[k]
        lc[0:32, cols] = jnp.where(inst == edge_inst, kernel_of(edge_col - rel), 0.0).astype(
            jnp.bfloat16
        )
        lc[32:128, cols] = jnp.zeros((96, 128), jnp.bfloat16)


def features_of(sums):
    density = sums[0:1]
    row = lax.broadcasted_iota(jnp.int32, sums.shape, 0)
    inverse = 1.0 / (1.0 + density)
    return jnp.where(row == 0, jnp.log1p(density), sums * inverse).astype(jnp.bfloat16)


def own_kernel(own_ref, table, s_own, s_edge, wt, ln, lc):
    build(own_ref, 0, (0, 1), table, wt, ln, lc)
    for half in range(2):
        for pair in range(2):
            rows = slice(pair * 256, (pair + 1) * 256)
            s_own[half, :, rows] = dot(wt[...], ln[half, rows, :], NT)
    s_edge[...] = dot(wt[...], lc[...], NT)


def near_kernel(near_ref, table, s_own, s_edge, f_near, edge_out, wt, ln, lc, s_near):
    side = lon_side()
    build(near_ref, (2 * side - 1) * CLON, (side,), table, wt, ln, lc)
    for pair in range(2):
        rows = slice(pair * 256, (pair + 1) * 256)
        s_near[:, rows] = dot(wt[...], ln[0, rows, :], NT)
    edge_out[...] = s_edge[...] + dot(wt[...], lc[...], NT)
    for i in range(EXT):
        rows = slice(i * SLOT, (i + 1) * SLOT)
        for k in range(INSTR):
            lanes = slice(k * 128, (k + 1) * 128)
            f_near[i * 128 + k * SLOT : i * 128 + (k + 1) * SLOT, :] = features_of(
                s_near[rows, lanes] + s_own[side, rows, lanes]
            )


def edge_features(sums):
    lane = lax.broadcasted_iota(jnp.int32, (SLOT, 128), 1)
    parts = [jnp.zeros((SLOT, 128), jnp.float32)] * INSTR
    for i in range(EXT):
        moved = sums[i * SLOT : (i + 1) * SLOT]
        if i > 0:
            moved = pltpu.roll(moved, EDGE * i, 1)
        for k in range(INSTR):
            place = lax.rem(lane - EDGE * (i + k) + 256, 128)
            parts[k] = jnp.where(place < EDGE, moved, parts[k])
    for k in range(1, INSTR):
        parts[k] = pltpu.roll(parts[k], 128 - EDGE * k, 1)
    return jnp.concatenate([features_of(part) for part in parts], axis=0)


def edge_terms(products):
    left = products[0][0:CHANNELS]
    right = products[0][2 * CHANNELS : 3 * CHANNELS]
    for a in (1, 2):
        left += pltpu.roll(products[a][0:CHANNELS], 128 - EDGE * a, 1)
        right += pltpu.roll(products[a][2 * CHANNELS : 3 * CHANNELS], 128 - EDGE * a, 1)
    lane = lax.broadcasted_iota(jnp.int32, left.shape, 1)
    return jnp.where(lax.rem(lane, EDGE) == 1, left, pltpu.roll(right, 128 - 4, 1))


def row_total(y, terms, row, bias):
    left = pltpu.roll(y[0:CHANNELS], 1, 1)
    right = pltpu.roll(y[2 * CHANNELS : 3 * CHANNELS], CLON - 1, 1)
    here = pltpu.roll(terms, 128 - (EDGE * row + 1), 1)
    lane = lax.broadcasted_iota(jnp.int32, here.shape, 1)
    middle = y[CHANNELS : 2 * CHANNELS] + bias
    return (
        middle[:, 0:128] + jnp.where(lane == 0, here, left[:, 0:128]) + right[:, 0:128],
        middle[:, 128:256] + left[:, 128:256] + jnp.where(lane == 127, here, right[:, 128:256]),
    )


def silu(x):
    return x / (1.0 + jnp.exp(-x))


def encode_kernel(
    far_ref, table, s_own, s_edge, f_near, w1_ref, w2_ref, w2_taps, b1_ref, b2_ref,
    out_ref, wt, ln, lc, s_far, feat, hid, stage, result, sems,
):
    lat_first = lax.axis_index("lat") * CLAT
    near_side = lon_side()
    side = 1 - near_side
    build(far_ref, (2 * side - 1) * CLON, (side,), table, wt, ln, lc)
    edge_sums = s_edge[...] + dot(wt[...], lc[...], NT)
    for pair in range(2):
        rows = slice(pair * 256, (pair + 1) * 256)
        s_far[:, rows] = dot(wt[...], ln[0, rows, :], NT)
    for i in range(EXT):
        rows = slice(i * SLOT, (i + 1) * SLOT)
        for k in range(INSTR):
            lanes = slice(k * 128, (k + 1) * 128)
            slot = slice(i * 128 + k * SLOT, i * 128 + (k + 1) * SLOT)
            far = features_of(s_far[rows, lanes] + s_own[side, rows, lanes])
            near = f_near[slot, :]
            feat[slot, 0:128] = jnp.where(near_side == 0, near, far)
            feat[slot, 128:256] = jnp.where(near_side == 0, far, near)

    w1 = w1_ref[...]
    b1 = b1_ref[...]
    edge_feat = edge_features(edge_sums)
    products = [dot(w1[:, a * 128 : (a + 1) * 128], edge_feat) for a in range(3)]
    terms = edge_terms(products)
    pre = b1
    for a in range(3):
        for b in range(3):
            part = products[a][b * CHANNELS : (b + 1) * CHANNELS]
            shift = (EDGE * a + b - 1) % 128
            pre = pre + (part if shift == 0 else pltpu.roll(part, 128 - shift, 1))
    lane_row = lax.broadcasted_iota(jnp.int32, (CHANNELS, 128), 1) // EDGE + lat_first - 1
    inside = (lane_row >= 0) & (lane_row < NLAT)
    edge_hid = jnp.where(inside, silu(pre), 0.0).astype(jnp.bfloat16)
    for h in range(HID):
        y = dot(w1, feat[h * 128 : (h + 3) * 128, :])
        row = lat_first - 1 + h
        for n, half in enumerate(row_total(y, terms, h, b1)):
            act = silu(half)
            if h in (0, HID - 1):
                act = jnp.where((row >= 0) & (row < NLAT), act, 0.0)
            hid[h * CHANNELS : (h + 1) * CHANNELS, n * 128 : (n + 1) * 128] = act.astype(jnp.bfloat16)

    w2 = w2_ref[...]
    b2 = b2_ref[...]
    terms = edge_terms([dot(w2_taps[a], edge_hid) for a in range(3)])
    size = CHANNELS * STEP
    for r in range(CLAT):
        y = dot(w2, hid[r * CHANNELS : (r + 3) * CHANNELS, :])
        for n, half in enumerate(row_total(y, terms, r, b2)):
            stage[pl.ds(n * size + r, CHANNELS, STEP), :] = half

    copies = []
    step = CHANNELS // PARTS
    for part in range(PARTS):
        channels = slice(part * step, (part + 1) * step)
        for n in range(2):
            for p in range(part * step, (part + 1) * step):
                result[p, :, n * 128 : (n + 1) * 128] = stage[
                    n * size + p * STEP : n * size + p * STEP + CLAT, :
                ].astype(jnp.bfloat16)
        copies.append(
            pltpu.make_async_copy(result.at[channels], out_ref.at[channels], sems.at[part])
        )
        copies[-1].start()
    for copy in copies:
        copy.wait()


def encode(near, own, far, w1, w2, w2_taps, b1, b2, table):
    vmem = pl.BlockSpec(memory_space=pltpu.VMEM)
    bf16, f32 = jnp.bfloat16, jnp.float32
    rows = EXT * SLOT
    s_own, s_edge = pl.pallas_call(
        own_kernel,
        out_shape=[
            jax.ShapeDtypeStruct((2, rows, INSTR * 128), f32),
            jax.ShapeDtypeStruct((rows, 128), f32),
        ],
        in_specs=[vmem] * 2,
        out_specs=[vmem] * 2,
        scratch_shapes=[
            pltpu.VMEM((rows, BAND), bf16),
            pltpu.VMEM((2, INSTR * 128, BAND), bf16),
            pltpu.VMEM((128, BAND), bf16),
        ],
        compiler_params=pltpu.CompilerParams(vmem_limit_bytes=16 * 1024 * 1024),
        cost_estimate=pl.CostEstimate(flops=2 * rows * BAND * 1152, bytes_accessed=3000000, transcendentals=0),
    )(own, table)
    f_near, s_edge = pl.pallas_call(
        near_kernel,
        out_shape=[
            jax.ShapeDtypeStruct((EXT * 128, 128), bf16),
            jax.ShapeDtypeStruct((rows, 128), f32),
        ],
        in_specs=[vmem] * 4,
        out_specs=[vmem] * 2,
        scratch_shapes=[
            pltpu.VMEM((rows, BAND), bf16),
            pltpu.VMEM((1, INSTR * 128, BAND), bf16),
            pltpu.VMEM((128, BAND), bf16),
            pltpu.VMEM((rows, INSTR * 128), f32),
        ],
        compiler_params=pltpu.CompilerParams(vmem_limit_bytes=16 * 1024 * 1024),
        cost_estimate=pl.CostEstimate(flops=2 * rows * BAND * 640, bytes_accessed=3000000, transcendentals=0),
    )(near, table, s_own, s_edge)
    return pl.pallas_call(
        encode_kernel,
        out_shape=jax.ShapeDtypeStruct((CHANNELS, CLAT, CLON), bf16),
        in_specs=[vmem] * 10,
        out_specs=pl.BlockSpec(memory_space=pl.ANY),
        scratch_shapes=[
            pltpu.VMEM((rows, BAND), bf16),
            pltpu.VMEM((1, INSTR * 128, BAND), bf16),
            pltpu.VMEM((128, BAND), bf16),
            pltpu.VMEM((rows, INSTR * 128), f32),
            pltpu.VMEM((EXT * 128, CLON), bf16),
            pltpu.VMEM((HID * CHANNELS, CLON), bf16),
            pltpu.VMEM((2 * CHANNELS * STEP, 128), f32),
            pltpu.VMEM((CHANNELS, CLAT, CLON), bf16),
            pltpu.SemaphoreType.DMA((PARTS,)),
        ],
        compiler_params=pltpu.CompilerParams(vmem_limit_bytes=24 * 1024 * 1024),
    )(far, table, s_own, s_edge, f_near, w1, w2, w2_taps, b1, b2)


def along(array, shape):
    return lax.broadcast_in_dim(array, shape, (len(shape) - 1,))


def pack(obs_values, obs_lat, obs_lon, instrument):
    shape = (SLOT, ROWS_DEV)
    row = lax.broadcasted_iota(jnp.int32, shape, 0)
    high = jnp.where(row == 0, along(obs_lat, shape), 0)
    ints = jnp.where(row == 31, along(obs_lon, shape), 0)
    ints = jnp.where(row == 0, along(instrument, shape), ints)
    return jnp.pad(obs_values, ((1, 1), (0, 0))) + (high * INSTR + ints).astype(jnp.float32)


def pack_small(b_first, b_second, scale):
    shape = (8, CHANNELS)
    row = lax.broadcasted_iota(jnp.int32, shape, 0)
    small = jnp.where(row == 2, along(scale, shape), 0.0)
    small = jnp.where(row == 1, along(b_second, shape), small)
    return jnp.where(row == 0, along(b_first, shape), small)


def arrange(w_first, w_second, small):
    bf16, f32 = jnp.bfloat16, jnp.float32
    wide = jnp.pad(w_second, ((0, 0), (0, 0), (CHANNELS, 0), (0, CIN - CHANNELS)))
    both = jnp.pad(w_first, ((0, 0), (0, 0), (0, CHANNELS), (0, 0))) + wide
    return pl.pallas_call(
        weights_kernel,
        out_shape=[
            jax.ShapeDtypeStruct((3 * CHANNELS, 3 * 128), bf16),
            jax.ShapeDtypeStruct((3 * CHANNELS, 3 * CHANNELS), bf16),
            jax.ShapeDtypeStruct((3, 3 * CHANNELS, CHANNELS), bf16),
            jax.ShapeDtypeStruct((CHANNELS, 1), f32),
            jax.ShapeDtypeStruct((CHANNELS, 1), f32),
            jax.ShapeDtypeStruct((2 * INSTR, 128), f32),
        ],
        in_specs=[pl.BlockSpec(memory_space=pltpu.VMEM)] * 2,
        out_specs=[pl.BlockSpec(memory_space=pltpu.VMEM)] * 6,
        compiler_params=pltpu.CompilerParams(vmem_limit_bytes=4 * 1024 * 1024),
        cost_estimate=pl.CostEstimate(flops=20000000, bytes_accessed=1000000, transcendentals=0),
    )(both, small)


def send(array, axis, target):
    peers = lax.axis_size(axis)
    return lax.ppermute(array, axis, [(i, target(i) % peers) for i in range(peers)])


def body(
    obs_values, obs_lat, obs_lon, instrument, length_scale, w_first, b_first, w_second, b_second
):
    rows = pack(obs_values, obs_lat, obs_lon, instrument)
    rows, length_scale = lax.optimization_barrier((rows, length_scale))
    scale = jnp.pad(length_scale, (0, CHANNELS - INSTR))
    others = send(rows, "lat", lambda i: i ^ 1)
    rows, others, scale, b_first, b_second, w_first, w_second = lax.optimization_barrier(
        (rows, others, scale, b_first, b_second, w_first, w_second)
    )
    rows = jnp.concatenate([rows, others], axis=1)
    rows, b_first, b_second, w_first, w_second = lax.optimization_barrier(
        (rows, b_first, b_second, w_first, w_second)
    )
    weights = arrange(w_first, w_second, pack_small(b_first, b_second, scale))
    others = send(rows, "lat", lambda i: i ^ 2)
    rows, others, weights = lax.optimization_barrier((rows, others, weights))
    rows = jnp.concatenate([rows, others], axis=1)
    across = send(rows, "lat", lambda i: i ^ 9)
    beside = send(rows, "lat", lambda i: i + 4 if i % 2 == 0 else i - 4)
    others = [across, send(beside, "lat", lambda i: i ^ 1), beside]
    rows = jnp.stack([rows] + others)
    near = send(rows, "lon", lambda i: i ^ 1)
    far = send(rows, "lon", lambda i: ((i + 1) ^ 1) - 1)
    return encode(near, rows, far, *weights)


def solution(mesh):
    return jax.shard_map(
        body,
        mesh=mesh,
        in_specs=(
            P(None, ("lat", "lon")),
            P(("lat", "lon")),
            P(("lat", "lon")),
            P(("lat", "lon")),
            P(),
            P(),
            P(),
            P(),
            P(),
        ),
        out_specs=P(None, "lat", "lon"),
        check_vma=False,
    )
```

```python
import jax
import jax.numpy as jnp
from jax import lax
from jax.experimental import pallas as pl
from jax.experimental.pallas import tpu as pltpu
from jax.sharding import PartitionSpec as P

CLAT = 16
CLON = 256
INSTR = 4
VALUES = 30
CHANNELS = 64
CIN = 124
SLOT = 32
NLAT = 256
NLON = 4096
ROWS_DEV = 32
STEP = 24
PARTS = 4
EXT = CLAT + 4
HID = CLAT + 2
EDGE = 6
BAND = 512
LOG2E = 1.4426950408889634
NT = (((1,), (1,)), ((), ()))
NN = (((1,), (0,)), ((), ()))


def dot(a, b, dims=NN):
    return lax.dot_general(a, b, dims, preferred_element_type=jnp.float32)


def fetch(sources, targets, sems):
    copies = [
        pltpu.make_async_copy(source, target, sems.at[n])
        for n, (source, target) in enumerate(zip(sources, targets, strict=True))
    ]
    for copy in copies:
        copy.start()
    for copy in copies:
        copy.wait()


def weights_kernel(both, small, w1, w2, w2_taps, b1, b2, table):
    source = lax.broadcasted_iota(jnp.int32, (CIN, 128), 0)
    slot = lax.broadcasted_iota(jnp.int32, (CIN, 128), 1)
    shifted = source
    for k in range(1, INSTR):
        slot = jnp.where(slot == SLOT * k - 1, -1, slot)
        shifted = shifted + jnp.where(source >= k * (VALUES + 1), 1, 0)
    spread = jnp.where(shifted == slot, 1.0, 0.0).astype(jnp.bfloat16)
    for a in range(3):
        for b in range(3):
            rows = slice(b * CHANNELS, (b + 1) * CHANNELS)
            first = both[a, b, 0:CHANNELS, :]
            second = both[a, b, CHANNELS : 2 * CHANNELS, 0:CHANNELS]
            w1[rows, a * 128 : (a + 1) * 128] = dot(first, spread).astype(jnp.bfloat16)
            w2[rows, a * CHANNELS : (a + 1) * CHANNELS] = second
            w2_taps[a, rows, :] = second
    up = lax.broadcasted_iota(jnp.int32, (CHANNELS, CHANNELS), 0)
    across = lax.broadcasted_iota(jnp.int32, (CHANNELS, CHANNELS), 1)
    for n, column in enumerate((b1, b2)):
        row = small[n : n + 1, 0:CHANNELS]
        column[...] = jnp.sum(jnp.where(up == across, row, 0.0), axis=1, keepdims=True)
    for k in range(INSTR):
        length = small[2:3, k : k + 1]
        reach = jnp.floor(4.0 * length)
        table[k : k + 1] = jnp.broadcast_to(-LOG2E * (0.5 / (length * length)), (1, 128))
        table[INSTR + k : INSTR + k + 1] = jnp.broadcast_to(reach * reach, (1, 128))


def lon_side():
    return 1 - lax.axis_index("lon") % 2


def build(ref, shift, halves, table, wt, ln, lc):
    lat_first = lax.axis_index("lat") * CLAT
    grid_row = lax.broadcasted_iota(jnp.int32, (24, 128), 0) + (lat_first - 2)
    row_ok = (grid_row >= 0) & (grid_row < NLAT)
    grid_row = grid_row.astype(jnp.float32)
    lane = lax.broadcasted_iota(jnp.int32, (128, 128), 0)
    edge = lax.broadcasted_iota(jnp.int32, (32, 128), 0)
    edge_inst = (edge // EDGE).astype(jnp.float32)
    edge = edge % EDGE
    edge_col = (edge - 2 + jnp.where(edge >= 3, CLON - 2, 0)).astype(jnp.float32)
    which = lax.broadcasted_iota(jnp.int32, (SLOT, 128), 0)
    for block in range(4):
        cols = slice(block * 128, (block + 1) * 128)
        data = ref[block]
        code = data[0:1].astype(jnp.int32)
        lat = (code // INSTR).astype(jnp.float32)
        inst = (code % INSTR).astype(jnp.float32)
        lon = data[31:32]
        rate = table[0:1]
        reach2 = table[INSTR : INSTR + 1]
        for k in range(1, INSTR):
            rate = jnp.where(inst == float(k), table[k : k + 1], rate)
            reach2 = jnp.where(inst == float(k), table[INSTR + k : INSTR + k + 1], reach2)
        rel = ((lon.astype(jnp.int32) & (CLON - 1)) + shift).astype(jnp.float32)

        def kernel_of(gap):
            gap2 = gap * gap
            return jnp.where(gap2 <= reach2, jnp.exp2(gap2 * rate), 0.0)

        lat_k = jnp.where(row_ok, kernel_of(grid_row - lat), 0.0)
        aug = jnp.where(which == 0, 1.0, jnp.where(which == 31, 0.0, data[0:SLOT]))
        for i in range(EXT):
            wt[i * SLOT : (i + 1) * SLOT, cols] = (lat_k[i : i + 1] * aug).astype(jnp.bfloat16)
        chosen = [jnp.where(inst == float(k), 1.0, 0.0).astype(jnp.bfloat16) for k in range(INSTR)]
        for n, half in enumerate(halves):
            ker = kernel_of((lane + half * 128).astype(jnp.float32) - rel).astype(jnp.bfloat16)
            for k in range(INSTR):
                ln[n, k * 128 : (k + 1) * 128, cols] = ker * chosen[k]
        lc[0:32, cols] = jnp.where(inst == edge_inst, kernel_of(edge_col - rel), 0.0).astype(
            jnp.bfloat16
        )
        lc[32:128, cols] = jnp.zeros((96, 128), jnp.bfloat16)


def features_of(sums):
    density = sums[0:1]
    row = lax.broadcasted_iota(jnp.int32, sums.shape, 0)
    inverse = 1.0 / (1.0 + density)
    return jnp.where(row == 0, jnp.log1p(density), sums * inverse).astype(jnp.bfloat16)


def own_kernel(own_ref, table, s_own, s_edge, wt, ln, lc):
    build(own_ref, 0, (0, 1), table, wt, ln, lc)
    for half in range(2):
        for pair in range(2):
            rows = slice(pair * 256, (pair + 1) * 256)
            s_own[half, :, rows] = dot(wt[...], ln[half, rows, :], NT)
    s_edge[...] = dot(wt[...], lc[...], NT)


def near_kernel(near_ref, table, s_own, s_edge, f_near, edge_out, wt, ln, lc, s_near):
    side = lon_side()
    build(near_ref, (2 * side - 1) * CLON, (side,), table, wt, ln, lc)
    for pair in range(2):
        rows = slice(pair * 256, (pair + 1) * 256)
        s_near[:, rows] = dot(wt[...], ln[0, rows, :], NT)
    edge_out[...] = s_edge[...] + dot(wt[...], lc[...], NT)
    for i in range(EXT):
        rows = slice(i * SLOT, (i + 1) * SLOT)
        for k in range(INSTR):
            lanes = slice(k * 128, (k + 1) * 128)
            f_near[i * 128 + k * SLOT : i * 128 + (k + 1) * SLOT, :] = features_of(
                s_near[rows, lanes] + s_own[side, rows, lanes]
            )


def edge_features(sums):
    lane = lax.broadcasted_iota(jnp.int32, (SLOT, 128), 1)
    parts = [jnp.zeros((SLOT, 128), jnp.float32)] * INSTR
    for i in range(EXT):
        moved = sums[i * SLOT : (i + 1) * SLOT]
        if i > 0:
            moved = pltpu.roll(moved, EDGE * i, 1)
        for k in range(INSTR):
            place = lax.rem(lane - EDGE * (i + k) + 256, 128)
            parts[k] = jnp.where(place < EDGE, moved, parts[k])
    for k in range(1, INSTR):
        parts[k] = pltpu.roll(parts[k], 128 - EDGE * k, 1)
    return jnp.concatenate([features_of(part) for part in parts], axis=0)


def edge_terms(products):
    left = products[0][0:CHANNELS]
    right = products[0][2 * CHANNELS : 3 * CHANNELS]
    for a in (1, 2):
        left += pltpu.roll(products[a][0:CHANNELS], 128 - EDGE * a, 1)
        right += pltpu.roll(products[a][2 * CHANNELS : 3 * CHANNELS], 128 - EDGE * a, 1)
    lane = lax.broadcasted_iota(jnp.int32, left.shape, 1)
    return jnp.where(lax.rem(lane, EDGE) == 1, left, pltpu.roll(right, 128 - 4, 1))


def row_total(y, terms, row, bias):
    left = pltpu.roll(y[0:CHANNELS], 1, 1)
    right = pltpu.roll(y[2 * CHANNELS : 3 * CHANNELS], CLON - 1, 1)
    here = pltpu.roll(terms, 128 - (EDGE * row + 1), 1)
    lane = lax.broadcasted_iota(jnp.int32, here.shape, 1)
    middle = y[CHANNELS : 2 * CHANNELS] + bias
    return (
        middle[:, 0:128] + jnp.where(lane == 0, here, left[:, 0:128]) + right[:, 0:128],
        middle[:, 128:256] + left[:, 128:256] + jnp.where(lane == 127, here, right[:, 128:256]),
    )


def silu(x):
    return x / (1.0 + jnp.exp(-x))


def encode_kernel(
    far_ref, table, s_own, s_edge, f_near, w1_ref, w2_ref, w2_taps, b1_ref, b2_ref,
    out_ref, wt, ln, lc, s_far, feat, hid, stage, result, sems,
):
    lat_first = lax.axis_index("lat") * CLAT
    near_side = lon_side()
    side = 1 - near_side
    build(far_ref, (2 * side - 1) * CLON, (side,), table, wt, ln, lc)
    edge_sums = s_edge[...] + dot(wt[...], lc[...], NT)
    for pair in range(2):
        rows = slice(pair * 256, (pair + 1) * 256)
        s_far[:, rows] = dot(wt[...], ln[0, rows, :], NT)
        for i in range(EXT):
            rows = slice(i * SLOT, (i + 1) * SLOT)
            for k in (2 * pair, 2 * pair + 1):
                lanes = slice(k * 128, (k + 1) * 128)
                slot = slice(i * 128 + k * SLOT, i * 128 + (k + 1) * SLOT)
                far = features_of(s_far[rows, lanes] + s_own[side, rows, lanes])
                near = f_near[slot, :]
                feat[slot, 0:128] = jnp.where(near_side == 0, near, far)
                feat[slot, 128:256] = jnp.where(near_side == 0, far, near)

    w1 = w1_ref[...]
    b1 = b1_ref[...]
    edge_feat = edge_features(edge_sums)
    products = [dot(w1[:, a * 128 : (a + 1) * 128], edge_feat) for a in range(3)]
    terms = edge_terms(products)
    pre = b1
    for a in range(3):
        for b in range(3):
            part = products[a][b * CHANNELS : (b + 1) * CHANNELS]
            shift = (EDGE * a + b - 1) % 128
            pre = pre + (part if shift == 0 else pltpu.roll(part, 128 - shift, 1))
    lane_row = lax.broadcasted_iota(jnp.int32, (CHANNELS, 128), 1) // EDGE + lat_first - 1
    inside = (lane_row >= 0) & (lane_row < NLAT)
    edge_hid = jnp.where(inside, silu(pre), 0.0).astype(jnp.bfloat16)
    for h in range(HID):
        y = dot(w1, feat[h * 128 : (h + 3) * 128, :])
        row = lat_first - 1 + h
        for n, half in enumerate(row_total(y, terms, h, b1)):
            act = silu(half)
            if h in (0, HID - 1):
                act = jnp.where((row >= 0) & (row < NLAT), act, 0.0)
            hid[h * CHANNELS : (h + 1) * CHANNELS, n * 128 : (n + 1) * 128] = act.astype(jnp.bfloat16)

    w2 = w2_ref[...]
    b2 = b2_ref[...]
    terms = edge_terms([dot(w2_taps[a], edge_hid) for a in range(3)])
    size = CHANNELS * STEP
    for r in range(CLAT):
        y = dot(w2, hid[r * CHANNELS : (r + 3) * CHANNELS, :])
        for n, half in enumerate(row_total(y, terms, r, b2)):
            stage[pl.ds(n * size + r, CHANNELS, STEP), :] = half

    copies = []
    step = CHANNELS // PARTS
    for part in range(PARTS):
        channels = slice(part * step, (part + 1) * step)
        for n in range(2):
            for p in range(part * step, (part + 1) * step):
                result[p, :, n * 128 : (n + 1) * 128] = stage[
                    n * size + p * STEP : n * size + p * STEP + CLAT, :
                ].astype(jnp.bfloat16)
        copies.append(
            pltpu.make_async_copy(result.at[channels], out_ref.at[channels], sems.at[part])
        )
        copies[-1].start()
    for copy in copies:
        copy.wait()


def encode(near, own, far, w1, w2, w2_taps, b1, b2, table):
    vmem = pl.BlockSpec(memory_space=pltpu.VMEM)
    bf16, f32 = jnp.bfloat16, jnp.float32
    rows = EXT * SLOT
    s_own, s_edge = pl.pallas_call(
        own_kernel,
        out_shape=[
            jax.ShapeDtypeStruct((2, rows, INSTR * 128), f32),
            jax.ShapeDtypeStruct((rows, 128), f32),
        ],
        in_specs=[vmem] * 2,
        out_specs=[vmem] * 2,
        scratch_shapes=[
            pltpu.VMEM((rows, BAND), bf16),
            pltpu.VMEM((2, INSTR * 128, BAND), bf16),
            pltpu.VMEM((128, BAND), bf16),
        ],
        compiler_params=pltpu.CompilerParams(vmem_limit_bytes=16 * 1024 * 1024),
        cost_estimate=pl.CostEstimate(flops=2 * rows * BAND * 1152, bytes_accessed=3000000, transcendentals=0),
    )(own, table)
    f_near, s_edge = pl.pallas_call(
        near_kernel,
        out_shape=[
            jax.ShapeDtypeStruct((EXT * 128, 128), bf16),
            jax.ShapeDtypeStruct((rows, 128), f32),
        ],
        in_specs=[vmem] * 4,
        out_specs=[vmem] * 2,
        scratch_shapes=[
            pltpu.VMEM((rows, BAND), bf16),
            pltpu.VMEM((1, INSTR * 128, BAND), bf16),
            pltpu.VMEM((128, BAND), bf16),
            pltpu.VMEM((rows, INSTR * 128), f32),
        ],
        compiler_params=pltpu.CompilerParams(vmem_limit_bytes=16 * 1024 * 1024),
        cost_estimate=pl.CostEstimate(flops=2 * rows * BAND * 640, bytes_accessed=3000000, transcendentals=0),
    )(near, table, s_own, s_edge)
    return pl.pallas_call(
        encode_kernel,
        out_shape=jax.ShapeDtypeStruct((CHANNELS, CLAT, CLON), bf16),
        in_specs=[vmem] * 10,
        out_specs=pl.BlockSpec(memory_space=pl.ANY),
        scratch_shapes=[
            pltpu.VMEM((rows, BAND), bf16),
            pltpu.VMEM((1, INSTR * 128, BAND), bf16),
            pltpu.VMEM((128, BAND), bf16),
            pltpu.VMEM((rows, INSTR * 128), f32),
            pltpu.VMEM((EXT * 128, CLON), bf16),
            pltpu.VMEM((HID * CHANNELS, CLON), bf16),
            pltpu.VMEM((2 * CHANNELS * STEP, 128), f32),
            pltpu.VMEM((CHANNELS, CLAT, CLON), bf16),
            pltpu.SemaphoreType.DMA((PARTS,)),
        ],
        compiler_params=pltpu.CompilerParams(vmem_limit_bytes=24 * 1024 * 1024),
    )(far, table, s_own, s_edge, f_near, w1, w2, w2_taps, b1, b2)


def along(array, shape):
    return lax.broadcast_in_dim(array, shape, (len(shape) - 1,))


def pack(obs_values, obs_lat, obs_lon, instrument):
    shape = (SLOT, ROWS_DEV)
    row = lax.broadcasted_iota(jnp.int32, shape, 0)
    high = jnp.where(row == 0, along(obs_lat, shape), 0)
    ints = jnp.where(row == 31, along(obs_lon, shape), 0)
    ints = jnp.where(row == 0, along(instrument, shape), ints)
    return jnp.pad(obs_values, ((1, 1), (0, 0))) + (high * INSTR + ints).astype(jnp.float32)


def pack_small(b_first, b_second, scale):
    shape = (8, CHANNELS)
    row = lax.broadcasted_iota(jnp.int32, shape, 0)
    small = jnp.where(row == 2, along(scale, shape), 0.0)
    small = jnp.where(row == 1, along(b_second, shape), small)
    return jnp.where(row == 0, along(b_first, shape), small)


def arrange(w_first, w_second, small):
    bf16, f32 = jnp.bfloat16, jnp.float32
    wide = jnp.pad(w_second, ((0, 0), (0, 0), (CHANNELS, 0), (0, CIN - CHANNELS)))
    both = jnp.pad(w_first, ((0, 0), (0, 0), (0, CHANNELS), (0, 0))) + wide
    return pl.pallas_call(
        weights_kernel,
        out_shape=[
            jax.ShapeDtypeStruct((3 * CHANNELS, 3 * 128), bf16),
            jax.ShapeDtypeStruct((3 * CHANNELS, 3 * CHANNELS), bf16),
            jax.ShapeDtypeStruct((3, 3 * CHANNELS, CHANNELS), bf16),
            jax.ShapeDtypeStruct((CHANNELS, 1), f32),
            jax.ShapeDtypeStruct((CHANNELS, 1), f32),
            jax.ShapeDtypeStruct((2 * INSTR, 128), f32),
        ],
        in_specs=[pl.BlockSpec(memory_space=pltpu.VMEM)] * 2,
        out_specs=[pl.BlockSpec(memory_space=pltpu.VMEM)] * 6,
        compiler_params=pltpu.CompilerParams(vmem_limit_bytes=4 * 1024 * 1024),
        cost_estimate=pl.CostEstimate(flops=20000000, bytes_accessed=1000000, transcendentals=0),
    )(both, small)


def send(array, axis, target):
    peers = lax.axis_size(axis)
    return lax.ppermute(array, axis, [(i, target(i) % peers) for i in range(peers)])


def body(
    obs_values, obs_lat, obs_lon, instrument, length_scale, w_first, b_first, w_second, b_second
):
    rows = pack(obs_values, obs_lat, obs_lon, instrument)
    rows, length_scale = lax.optimization_barrier((rows, length_scale))
    scale = jnp.pad(length_scale, (0, CHANNELS - INSTR))
    others = send(rows, "lat", lambda i: i ^ 1)
    rows, others, scale, b_first, b_second, w_first, w_second = lax.optimization_barrier(
        (rows, others, scale, b_first, b_second, w_first, w_second)
    )
    rows = jnp.concatenate([rows, others], axis=1)
    rows, b_first, b_second, w_first, w_second = lax.optimization_barrier(
        (rows, b_first, b_second, w_first, w_second)
    )
    weights = arrange(w_first, w_second, pack_small(b_first, b_second, scale))
    others = send(rows, "lat", lambda i: i ^ 2)
    rows, others, weights = lax.optimization_barrier((rows, others, weights))
    rows = jnp.concatenate([rows, others], axis=1)
    across = send(rows, "lat", lambda i: i ^ 9)
    beside = send(rows, "lat", lambda i: i + 4 if i % 2 == 0 else i - 4)
    others = [across, send(beside, "lat", lambda i: i ^ 1), beside]
    rows = jnp.stack([rows] + others)
    near = send(rows, "lon", lambda i: i ^ 1)
    far = send(rows, "lon", lambda i: ((i + 1) ^ 1) - 1)
    return encode(near, rows, far, *weights)


def solution(mesh):
    return jax.shard_map(
        body,
        mesh=mesh,
        in_specs=(
            P(None, ("lat", "lon")),
            P(("lat", "lon")),
            P(("lat", "lon")),
            P(("lat", "lon")),
            P(),
            P(),
            P(),
            P(),
            P(),
        ),
        out_specs=P(None, "lat", "lon"),
        check_vma=False,
    )
```

```python
import jax
import jax.numpy as jnp
from jax import lax
from jax.experimental import pallas as pl
from jax.experimental.pallas import tpu as pltpu
from jax.sharding import PartitionSpec as P

CLAT = 16
CLON = 256
INSTR = 4
VALUES = 30
CHANNELS = 64
CIN = 124
SLOT = 32
NLAT = 256
NLON = 4096
ROWS_DEV = 32
STEP = 24
PARTS = 8
EXT = CLAT + 4
HID = CLAT + 2
EDGE = 6
BAND = 512
LOG2E = 1.4426950408889634
NT = (((1,), (1,)), ((), ()))
NN = (((1,), (0,)), ((), ()))


def dot(a, b, dims=NN):
    return lax.dot_general(a, b, dims, preferred_element_type=jnp.float32)


def fetch(sources, targets, sems):
    copies = [
        pltpu.make_async_copy(source, target, sems.at[n])
        for n, (source, target) in enumerate(zip(sources, targets, strict=True))
    ]
    for copy in copies:
        copy.start()
    for copy in copies:
        copy.wait()


def weights_kernel(both, small, w1, w2, w2_taps, b1, b2, table):
    source = lax.broadcasted_iota(jnp.int32, (CIN, 128), 0)
    slot = lax.broadcasted_iota(jnp.int32, (CIN, 128), 1)
    shifted = source
    for k in range(1, INSTR):
        slot = jnp.where(slot == SLOT * k - 1, -1, slot)
        shifted = shifted + jnp.where(source >= k * (VALUES + 1), 1, 0)
    spread = jnp.where(shifted == slot, 1.0, 0.0).astype(jnp.bfloat16)
    for a in range(3):
        for b in range(3):
            rows = slice(b * CHANNELS, (b + 1) * CHANNELS)
            first = both[a, b, 0:CHANNELS, :]
            second = both[a, b, CHANNELS : 2 * CHANNELS, 0:CHANNELS]
            w1[rows, a * 128 : (a + 1) * 128] = dot(first, spread).astype(jnp.bfloat16)
            w2[rows, a * CHANNELS : (a + 1) * CHANNELS] = second
            w2_taps[a, rows, :] = second
    up = lax.broadcasted_iota(jnp.int32, (CHANNELS, CHANNELS), 0)
    across = lax.broadcasted_iota(jnp.int32, (CHANNELS, CHANNELS), 1)
    for n, column in enumerate((b1, b2)):
        row = small[n : n + 1, 0:CHANNELS]
        column[...] = jnp.sum(jnp.where(up == across, row, 0.0), axis=1, keepdims=True)
    for k in range(INSTR):
        length = small[2:3, k : k + 1]
        reach = jnp.floor(4.0 * length)
        table[k : k + 1] = jnp.broadcast_to(-LOG2E * (0.5 / (length * length)), (1, 128))
        table[INSTR + k : INSTR + k + 1] = jnp.broadcast_to(reach * reach, (1, 128))


def lon_side():
    return 1 - lax.axis_index("lon") % 2


def build(ref, shift, halves, table, wt, ln, lc):
    lat_first = lax.axis_index("lat") * CLAT
    grid_row = lax.broadcasted_iota(jnp.int32, (24, 128), 0) + (lat_first - 2)
    row_ok = (grid_row >= 0) & (grid_row < NLAT)
    grid_row = grid_row.astype(jnp.float32)
    lane = lax.broadcasted_iota(jnp.int32, (128, 128), 0)
    edge = lax.broadcasted_iota(jnp.int32, (32, 128), 0)
    edge_inst = (edge // EDGE).astype(jnp.float32)
    edge = edge % EDGE
    edge_col = (edge - 2 + jnp.where(edge >= 3, CLON - 2, 0)).astype(jnp.float32)
    which = lax.broadcasted_iota(jnp.int32, (SLOT, 128), 0)
    for block in range(4):
        cols = slice(block * 128, (block + 1) * 128)
        data = ref[block]
        code = data[0:1].astype(jnp.int32)
        lat = (code // INSTR).astype(jnp.float32)
        inst = (code % INSTR).astype(jnp.float32)
        lon = data[31:32]
        rate = table[0:1]
        reach2 = table[INSTR : INSTR + 1]
        for k in range(1, INSTR):
            rate = jnp.where(inst == float(k), table[k : k + 1], rate)
            reach2 = jnp.where(inst == float(k), table[INSTR + k : INSTR + k + 1], reach2)
        rel = ((lon.astype(jnp.int32) & (CLON - 1)) + shift).astype(jnp.float32)

        def kernel_of(gap):
            gap2 = gap * gap
            return jnp.where(gap2 <= reach2, jnp.exp2(gap2 * rate), 0.0)

        lat_k = jnp.where(row_ok, kernel_of(grid_row - lat), 0.0)
        aug = jnp.where(which == 0, 1.0, jnp.where(which == 31, 0.0, data[0:SLOT]))
        for i in range(EXT):
            wt[i * SLOT : (i + 1) * SLOT, cols] = (lat_k[i : i + 1] * aug).astype(jnp.bfloat16)
        chosen = [jnp.where(inst == float(k), 1.0, 0.0).astype(jnp.bfloat16) for k in range(INSTR)]
        for n, half in enumerate(halves):
            ker = kernel_of((lane + half * 128).astype(jnp.float32) - rel).astype(jnp.bfloat16)
            for k in range(INSTR):
                ln[n, k * 128 : (k + 1) * 128, cols] = ker * chosen[k]
        lc[0:32, cols] = jnp.where(inst == edge_inst, kernel_of(edge_col - rel), 0.0).astype(
            jnp.bfloat16
        )
        lc[32:128, cols] = jnp.zeros((96, 128), jnp.bfloat16)


def features_of(sums):
    density = sums[0:1]
    row = lax.broadcasted_iota(jnp.int32, sums.shape, 0)
    inverse = 1.0 / (1.0 + density)
    return jnp.where(row == 0, jnp.log1p(density), sums * inverse).astype(jnp.bfloat16)


def own_kernel(own_ref, table, s_own, s_edge, wt, ln, lc):
    build(own_ref, 0, (0, 1), table, wt, ln, lc)
    for half in range(2):
        for pair in range(2):
            rows = slice(pair * 256, (pair + 1) * 256)
            s_own[half, :, rows] = dot(wt[...], ln[half, rows, :], NT)
    s_edge[...] = dot(wt[...], lc[...], NT)


def near_kernel(near_ref, table, s_own, s_edge, f_near, edge_out, wt, ln, lc, s_near):
    side = lon_side()
    build(near_ref, (2 * side - 1) * CLON, (side,), table, wt, ln, lc)
    for pair in range(2):
        rows = slice(pair * 256, (pair + 1) * 256)
        s_near[:, rows] = dot(wt[...], ln[0, rows, :], NT)
    edge_out[...] = s_edge[...] + dot(wt[...], lc[...], NT)
    for i in range(EXT):
        rows = slice(i * SLOT, (i + 1) * SLOT)
        for k in range(INSTR):
            lanes = slice(k * 128, (k + 1) * 128)
            f_near[i * 128 + k * SLOT : i * 128 + (k + 1) * SLOT, :] = features_of(
                s_near[rows, lanes] + s_own[side, rows, lanes]
            )


def edge_features(sums):
    lane = lax.broadcasted_iota(jnp.int32, (SLOT, 128), 1)
    parts = [jnp.zeros((SLOT, 128), jnp.float32)] * INSTR
    for i in range(EXT):
        moved = sums[i * SLOT : (i + 1) * SLOT]
        if i > 0:
            moved = pltpu.roll(moved, EDGE * i, 1)
        for k in range(INSTR):
            place = lax.rem(lane - EDGE * (i + k) + 256, 128)
            parts[k] = jnp.where(place < EDGE, moved, parts[k])
    for k in range(1, INSTR):
        parts[k] = pltpu.roll(parts[k], 128 - EDGE * k, 1)
    return jnp.concatenate([features_of(part) for part in parts], axis=0)


def edge_terms(products):
    left = products[0][0:CHANNELS]
    right = products[0][2 * CHANNELS : 3 * CHANNELS]
    for a in (1, 2):
        left += pltpu.roll(products[a][0:CHANNELS], 128 - EDGE * a, 1)
        right += pltpu.roll(products[a][2 * CHANNELS : 3 * CHANNELS], 128 - EDGE * a, 1)
    lane = lax.broadcasted_iota(jnp.int32, left.shape, 1)
    return jnp.where(lax.rem(lane, EDGE) == 1, left, pltpu.roll(right, 128 - 4, 1))


def row_total(y, terms, row, bias):
    halves = (slice(0, 128), slice(128, 256))
    here = pltpu.roll(terms, 128 - (EDGE * row + 1), 1)
    lane = lax.broadcasted_iota(jnp.int32, here.shape, 1)
    left = [pltpu.roll(y[0:CHANNELS, half], 1, 1) for half in halves]
    right = [pltpu.roll(y[2 * CHANNELS : 3 * CHANNELS, half], 127, 1) for half in halves]
    middle = [y[CHANNELS : 2 * CHANNELS, half] + bias for half in halves]
    return (
        middle[0] + jnp.where(lane == 0, here, left[0]) + jnp.where(lane == 127, right[1], right[0]),
        middle[1] + jnp.where(lane == 0, left[0], left[1]) + jnp.where(lane == 127, here, right[1]),
    )


def silu(x):
    return x / (1.0 + jnp.exp(-x))


def encode_kernel(
    far_ref, table, s_own, s_edge, f_near, w1_ref, w2_ref, w2_taps, b1_ref, b2_ref,
    out_ref, wt, ln, lc, s_far, feat, hid, stage, result, sems,
):
    lat_first = lax.axis_index("lat") * CLAT
    near_side = lon_side()
    side = 1 - near_side
    build(far_ref, (2 * side - 1) * CLON, (side,), table, wt, ln, lc)
    edge_sums = s_edge[...] + dot(wt[...], lc[...], NT)
    for pair in range(2):
        rows = slice(pair * 256, (pair + 1) * 256)
        s_far[:, rows] = dot(wt[...], ln[0, rows, :], NT)
    for i in range(EXT):
        rows = slice(i * SLOT, (i + 1) * SLOT)
        for k in range(INSTR):
            lanes = slice(k * 128, (k + 1) * 128)
            slot = slice(i * 128 + k * SLOT, i * 128 + (k + 1) * SLOT)
            far = features_of(s_far[rows, lanes] + s_own[side, rows, lanes])
            near = f_near[slot, :]
            feat[slot, 0:128] = jnp.where(near_side == 0, near, far)
            feat[slot, 128:256] = jnp.where(near_side == 0, far, near)

    w1 = w1_ref[...]
    b1 = b1_ref[...]
    edge_feat = edge_features(edge_sums)
    products = [dot(w1[:, a * 128 : (a + 1) * 128], edge_feat) for a in range(3)]
    terms = edge_terms(products)
    pre = b1
    for a in range(3):
        for b in range(3):
            part = products[a][b * CHANNELS : (b + 1) * CHANNELS]
            shift = (EDGE * a + b - 1) % 128
            pre = pre + (part if shift == 0 else pltpu.roll(part, 128 - shift, 1))
    lane_row = lax.broadcasted_iota(jnp.int32, (CHANNELS, 128), 1) // EDGE + lat_first - 1
    inside = (lane_row >= 0) & (lane_row < NLAT)
    edge_hid = jnp.where(inside, silu(pre), 0.0).astype(jnp.bfloat16)
    for h in range(HID):
        y = dot(w1, feat[h * 128 : (h + 3) * 128, :])
        row = lat_first - 1 + h
        for n, half in enumerate(row_total(y, terms, h, b1)):
            act = silu(half)
            if h in (0, HID - 1):
                act = jnp.where((row >= 0) & (row < NLAT), act, 0.0)
            hid[h * CHANNELS : (h + 1) * CHANNELS, n * 128 : (n + 1) * 128] = act.astype(jnp.bfloat16)

    w2 = w2_ref[...]
    b2 = b2_ref[...]
    terms = edge_terms([dot(w2_taps[a], edge_hid) for a in range(3)])
    size = CHANNELS * STEP
    for r in range(CLAT):
        y = dot(w2, hid[r * CHANNELS : (r + 3) * CHANNELS, :])
        for n, half in enumerate(row_total(y, terms, r, b2)):
            stage[pl.ds(n * size + r, CHANNELS, STEP), :] = half

    copies = []
    step = CHANNELS // PARTS
    for part in range(PARTS):
        channels = slice(part * step, (part + 1) * step)
        for n in range(2):
            for p in range(part * step, (part + 1) * step):
                result[p, :, n * 128 : (n + 1) * 128] = stage[
                    n * size + p * STEP : n * size + p * STEP + CLAT, :
                ].astype(jnp.bfloat16)
        copies.append(
            pltpu.make_async_copy(result.at[channels], out_ref.at[channels], sems.at[part])
        )
        copies[-1].start()
    for copy in copies:
        copy.wait()


def encode(near, own, far, w1, w2, w2_taps, b1, b2, table):
    vmem = pl.BlockSpec(memory_space=pltpu.VMEM)
    bf16, f32 = jnp.bfloat16, jnp.float32
    rows = EXT * SLOT
    s_own, s_edge = pl.pallas_call(
        own_kernel,
        out_shape=[
            jax.ShapeDtypeStruct((2, rows, INSTR * 128), f32),
            jax.ShapeDtypeStruct((rows, 128), f32),
        ],
        in_specs=[vmem] * 2,
        out_specs=[vmem] * 2,
        scratch_shapes=[
            pltpu.VMEM((rows, BAND), bf16),
            pltpu.VMEM((2, INSTR * 128, BAND), bf16),
            pltpu.VMEM((128, BAND), bf16),
        ],
        compiler_params=pltpu.CompilerParams(vmem_limit_bytes=16 * 1024 * 1024),
        cost_estimate=pl.CostEstimate(flops=2 * rows * BAND * 1152, bytes_accessed=3000000, transcendentals=0),
    )(own, table)
    f_near, s_edge = pl.pallas_call(
        near_kernel,
        out_shape=[
            jax.ShapeDtypeStruct((EXT * 128, 128), bf16),
            jax.ShapeDtypeStruct((rows, 128), f32),
        ],
        in_specs=[vmem] * 4,
        out_specs=[vmem] * 2,
        scratch_shapes=[
            pltpu.VMEM((rows, BAND), bf16),
            pltpu.VMEM((1, INSTR * 128, BAND), bf16),
            pltpu.VMEM((128, BAND), bf16),
            pltpu.VMEM((rows, INSTR * 128), f32),
        ],
        compiler_params=pltpu.CompilerParams(vmem_limit_bytes=16 * 1024 * 1024),
        cost_estimate=pl.CostEstimate(flops=2 * rows * BAND * 640, bytes_accessed=3000000, transcendentals=0),
    )(near, table, s_own, s_edge)
    return pl.pallas_call(
        encode_kernel,
        out_shape=jax.ShapeDtypeStruct((CHANNELS, CLAT, CLON), bf16),
        in_specs=[vmem] * 10,
        out_specs=pl.BlockSpec(memory_space=pl.ANY),
        scratch_shapes=[
            pltpu.VMEM((rows, BAND), bf16),
            pltpu.VMEM((1, INSTR * 128, BAND), bf16),
            pltpu.VMEM((128, BAND), bf16),
            pltpu.VMEM((rows, INSTR * 128), f32),
            pltpu.VMEM((EXT * 128, CLON), bf16),
            pltpu.VMEM((HID * CHANNELS, CLON), bf16),
            pltpu.VMEM((2 * CHANNELS * STEP, 128), f32),
            pltpu.VMEM((CHANNELS, CLAT, CLON), bf16),
            pltpu.SemaphoreType.DMA((PARTS,)),
        ],
        compiler_params=pltpu.CompilerParams(vmem_limit_bytes=24 * 1024 * 1024),
    )(far, table, s_own, s_edge, f_near, w1, w2, w2_taps, b1, b2)


def along(array, shape):
    return lax.broadcast_in_dim(array, shape, (len(shape) - 1,))


def pack(obs_values, obs_lat, obs_lon, instrument):
    shape = (SLOT, ROWS_DEV)
    row = lax.broadcasted_iota(jnp.int32, shape, 0)
    high = jnp.where(row == 0, along(obs_lat, shape), 0)
    ints = jnp.where(row == 31, along(obs_lon, shape), 0)
    ints = jnp.where(row == 0, along(instrument, shape), ints)
    return jnp.pad(obs_values, ((1, 1), (0, 0))) + (high * INSTR + ints).astype(jnp.float32)


def pack_small(b_first, b_second, scale):
    shape = (8, CHANNELS)
    row = lax.broadcasted_iota(jnp.int32, shape, 0)
    small = jnp.where(row == 2, along(scale, shape), 0.0)
    small = jnp.where(row == 1, along(b_second, shape), small)
    return jnp.where(row == 0, along(b_first, shape), small)


def arrange(w_first, w_second, small):
    bf16, f32 = jnp.bfloat16, jnp.float32
    wide = jnp.pad(w_second, ((0, 0), (0, 0), (CHANNELS, 0), (0, CIN - CHANNELS)))
    both = jnp.pad(w_first, ((0, 0), (0, 0), (0, CHANNELS), (0, 0))) + wide
    return pl.pallas_call(
        weights_kernel,
        out_shape=[
            jax.ShapeDtypeStruct((3 * CHANNELS, 3 * 128), bf16),
            jax.ShapeDtypeStruct((3 * CHANNELS, 3 * CHANNELS), bf16),
            jax.ShapeDtypeStruct((3, 3 * CHANNELS, CHANNELS), bf16),
            jax.ShapeDtypeStruct((CHANNELS, 1), f32),
            jax.ShapeDtypeStruct((CHANNELS, 1), f32),
            jax.ShapeDtypeStruct((2 * INSTR, 128), f32),
        ],
        in_specs=[pl.BlockSpec(memory_space=pltpu.VMEM)] * 2,
        out_specs=[pl.BlockSpec(memory_space=pltpu.VMEM)] * 6,
        compiler_params=pltpu.CompilerParams(vmem_limit_bytes=4 * 1024 * 1024),
        cost_estimate=pl.CostEstimate(flops=20000000, bytes_accessed=1000000, transcendentals=0),
    )(both, small)


def send(array, axis, target):
    peers = lax.axis_size(axis)
    return lax.ppermute(array, axis, [(i, target(i) % peers) for i in range(peers)])


def body(
    obs_values, obs_lat, obs_lon, instrument, length_scale, w_first, b_first, w_second, b_second
):
    rows = pack(obs_values, obs_lat, obs_lon, instrument)
    rows, length_scale = lax.optimization_barrier((rows, length_scale))
    scale = jnp.pad(length_scale, (0, CHANNELS - INSTR))
    others = send(rows, "lat", lambda i: i ^ 1)
    rows, others, scale, b_first, b_second, w_first, w_second = lax.optimization_barrier(
        (rows, others, scale, b_first, b_second, w_first, w_second)
    )
    rows = jnp.concatenate([rows, others], axis=1)
    rows, b_first, b_second, w_first, w_second = lax.optimization_barrier(
        (rows, b_first, b_second, w_first, w_second)
    )
    weights = arrange(w_first, w_second, pack_small(b_first, b_second, scale))
    others = send(rows, "lat", lambda i: i ^ 2)
    rows, others, weights = lax.optimization_barrier((rows, others, weights))
    rows = jnp.concatenate([rows, others], axis=1)
    across = send(rows, "lat", lambda i: i ^ 9)
    beside = send(rows, "lat", lambda i: i + 4 if i % 2 == 0 else i - 4)
    others = [across, send(beside, "lat", lambda i: i ^ 1), beside]
    rows = jnp.stack([rows] + others)
    near = send(rows, "lon", lambda i: i ^ 1)
    far = send(rows, "lon", lambda i: ((i + 1) ^ 1) - 1)
    return encode(near, rows, far, *weights)


def solution(mesh):
    return jax.shard_map(
        body,
        mesh=mesh,
        in_specs=(
            P(None, ("lat", "lon")),
            P(("lat", "lon")),
            P(("lat", "lon")),
            P(("lat", "lon")),
            P(),
            P(),
            P(),
            P(),
            P(),
        ),
        out_specs=P(None, "lat", "lon"),
        check_vma=False,
    )
```

```python
import jax
import jax.numpy as jnp
from jax import lax
from jax.experimental import pallas as pl
from jax.experimental.pallas import tpu as pltpu
from jax.sharding import PartitionSpec as P

CLAT = 16
CLON = 256
INSTR = 4
VALUES = 30
CHANNELS = 64
CIN = 124
SLOT = 32
NLAT = 256
NLON = 4096
ROWS_DEV = 32
STEP = 24
PARTS = 8
EXT = CLAT + 4
HID = CLAT + 2
EDGE = 6
BAND = 512
LOG2E = 1.4426950408889634
NT = (((1,), (1,)), ((), ()))
NN = (((1,), (0,)), ((), ()))


def dot(a, b, dims=NN):
    return lax.dot_general(a, b, dims, preferred_element_type=jnp.float32)


def fetch(sources, targets, sems):
    copies = [
        pltpu.make_async_copy(source, target, sems.at[n])
        for n, (source, target) in enumerate(zip(sources, targets, strict=True))
    ]
    for copy in copies:
        copy.start()
    for copy in copies:
        copy.wait()


def weights_kernel(both, small, w1, w2, w2_taps, b1, b2, table):
    source = lax.broadcasted_iota(jnp.int32, (CIN, 128), 0)
    slot = lax.broadcasted_iota(jnp.int32, (CIN, 128), 1)
    shifted = source
    for k in range(1, INSTR):
        slot = jnp.where(slot == SLOT * k - 1, -1, slot)
        shifted = shifted + jnp.where(source >= k * (VALUES + 1), 1, 0)
    spread = jnp.where(shifted == slot, 1.0, 0.0).astype(jnp.bfloat16)
    for a in range(3):
        for b in range(3):
            rows = slice(b * CHANNELS, (b + 1) * CHANNELS)
            first = both[a, b, 0:CHANNELS, :]
            second = both[a, b, CHANNELS : 2 * CHANNELS, 0:CHANNELS]
            w1[rows, a * 128 : (a + 1) * 128] = dot(first, spread).astype(jnp.bfloat16)
            w2[rows, a * CHANNELS : (a + 1) * CHANNELS] = second
            w2_taps[a, rows, :] = second
    up = lax.broadcasted_iota(jnp.int32, (CHANNELS, CHANNELS), 0)
    across = lax.broadcasted_iota(jnp.int32, (CHANNELS, CHANNELS), 1)
    for n, column in enumerate((b1, b2)):
        row = small[n : n + 1, 0:CHANNELS]
        column[...] = jnp.sum(jnp.where(up == across, row, 0.0), axis=1, keepdims=True)
    for k in range(INSTR):
        length = small[2:3, k : k + 1]
        reach = jnp.floor(4.0 * length)
        table[k : k + 1] = jnp.broadcast_to(-LOG2E * (0.5 / (length * length)), (1, 128))
        table[INSTR + k : INSTR + k + 1] = jnp.broadcast_to(reach * reach, (1, 128))


def lon_side():
    return 1 - lax.axis_index("lon") % 2


def build(ref, shift, halves, table, wt, ln, lc):
    lat_first = lax.axis_index("lat") * CLAT
    grid_row = lax.broadcasted_iota(jnp.int32, (24, 128), 0) + (lat_first - 2)
    row_ok = (grid_row >= 0) & (grid_row < NLAT)
    grid_row = grid_row.astype(jnp.float32)
    lane = lax.broadcasted_iota(jnp.int32, (128, 128), 0)
    edge = lax.broadcasted_iota(jnp.int32, (32, 128), 0)
    edge_inst = (edge // EDGE).astype(jnp.float32)
    edge = edge % EDGE
    edge_col = (edge - 2 + jnp.where(edge >= 3, CLON - 2, 0)).astype(jnp.float32)
    which = lax.broadcasted_iota(jnp.int32, (SLOT, 128), 0)
    for block in range(4):
        cols = slice(block * 128, (block + 1) * 128)
        data = ref[block]
        code = data[0:1].astype(jnp.int32)
        lat = (code // INSTR).astype(jnp.float32)
        inst = (code % INSTR).astype(jnp.float32)
        lon = data[31:32]
        rate = table[0:1]
        reach2 = table[INSTR : INSTR + 1]
        for k in range(1, INSTR):
            rate = jnp.where(inst == float(k), table[k : k + 1], rate)
            reach2 = jnp.where(inst == float(k), table[INSTR + k : INSTR + k + 1], reach2)
        rel = ((lon.astype(jnp.int32) & (CLON - 1)) + shift).astype(jnp.float32)

        def kernel_of(gap):
            gap2 = gap * gap
            return jnp.where(gap2 <= reach2, jnp.exp2(gap2 * rate), 0.0)

        lat_k = jnp.where(row_ok, kernel_of(grid_row - lat), 0.0)
        aug = jnp.where(which == 0, 1.0, jnp.where(which == 31, 0.0, data[0:SLOT]))
        for i in range(EXT):
            wt[i * SLOT : (i + 1) * SLOT, cols] = (lat_k[i : i + 1] * aug).astype(jnp.bfloat16)
        chosen = [jnp.where(inst == float(k), 1.0, 0.0).astype(jnp.bfloat16) for k in range(INSTR)]
        for n, half in enumerate(halves):
            ker = kernel_of((lane + half * 128).astype(jnp.float32) - rel).astype(jnp.bfloat16)
            for k in range(INSTR):
                ln[n, k * 128 : (k + 1) * 128, cols] = ker * chosen[k]
        lc[0:32, cols] = jnp.where(inst == edge_inst, kernel_of(edge_col - rel), 0.0).astype(
            jnp.bfloat16
        )
        lc[32:128, cols] = jnp.zeros((96, 128), jnp.bfloat16)


def features_of(sums):
    density = sums[0:1]
    row = lax.broadcasted_iota(jnp.int32, sums.shape, 0)
    inverse = 1.0 / (1.0 + density)
    return jnp.where(row == 0, jnp.log1p(density), sums * inverse).astype(jnp.bfloat16)


def own_kernel(own_ref, table, s_own, s_edge, wt, ln, lc):
    build(own_ref, 0, (0, 1), table, wt, ln, lc)
    for half in range(2):
        for pair in range(2):
            rows = slice(pair * 256, (pair + 1) * 256)
            s_own[half, :, rows] = dot(wt[...], ln[half, rows, :], NT)
    s_edge[...] = dot(wt[...], lc[...], NT)


def near_kernel(near_ref, table, s_own, s_edge, f_near, edge_out, wt, ln, lc, s_near):
    side = lon_side()
    build(near_ref, (2 * side - 1) * CLON, (side,), table, wt, ln, lc)
    for pair in range(2):
        rows = slice(pair * 256, (pair + 1) * 256)
        s_near[:, rows] = dot(wt[...], ln[0, rows, :], NT)
    edge_out[...] = s_edge[...] + dot(wt[...], lc[...], NT)
    for i in range(EXT):
        rows = slice(i * SLOT, (i + 1) * SLOT)
        for k in range(INSTR):
            lanes = slice(k * 128, (k + 1) * 128)
            f_near[i * 128 + k * SLOT : i * 128 + (k + 1) * SLOT, :] = features_of(
                s_near[rows, lanes] + s_own[side, rows, lanes]
            )


def edge_features(sums):
    lane = lax.broadcasted_iota(jnp.int32, (SLOT, 128), 1)
    parts = [jnp.zeros((SLOT, 128), jnp.float32)] * INSTR
    for i in range(EXT):
        moved = sums[i * SLOT : (i + 1) * SLOT]
        if i > 0:
            moved = pltpu.roll(moved, EDGE * i, 1)
        for k in range(INSTR):
            place = lax.rem(lane - EDGE * (i + k) + 256, 128)
            parts[k] = jnp.where(place < EDGE, moved, parts[k])
    for k in range(1, INSTR):
        parts[k] = pltpu.roll(parts[k], 128 - EDGE * k, 1)
    return jnp.concatenate([features_of(part) for part in parts], axis=0)


def edge_terms(products):
    left = products[0][0:CHANNELS]
    right = products[0][2 * CHANNELS : 3 * CHANNELS]
    for a in (1, 2):
        left += pltpu.roll(products[a][0:CHANNELS], 128 - EDGE * a, 1)
        right += pltpu.roll(products[a][2 * CHANNELS : 3 * CHANNELS], 128 - EDGE * a, 1)
    lane = lax.broadcasted_iota(jnp.int32, left.shape, 1)
    return jnp.where(lax.rem(lane, EDGE) == 1, left, pltpu.roll(right, 128 - 4, 1))


def row_total(y, terms, row, bias):
    halves = (slice(0, 128), slice(128, 256))
    here = pltpu.roll(terms, 128 - (EDGE * row + 1), 1)
    lane = lax.broadcasted_iota(jnp.int32, here.shape, 1)
    left = [pltpu.roll(y[0:CHANNELS, half], 1, 1) for half in halves]
    right = [pltpu.roll(y[2 * CHANNELS : 3 * CHANNELS, half], 127, 1) for half in halves]
    middle = [y[CHANNELS : 2 * CHANNELS, half] + bias for half in halves]
    return (
        middle[0] + jnp.where(lane == 0, here, left[0]) + jnp.where(lane == 127, right[1], right[0]),
        middle[1] + jnp.where(lane == 0, left[0], left[1]) + jnp.where(lane == 127, here, right[1]),
    )


def silu(x):
    return x / (1.0 + jnp.exp(-x))


def encode_kernel(
    far_ref, table, s_own, s_edge, f_near, w1_ref, w2_ref, w2_taps, b1_ref, b2_ref,
    out_ref, wt, ln, lc, s_far, feat, hid, stage, result, sems,
):
    lat_first = lax.axis_index("lat") * CLAT
    near_side = lon_side()
    side = 1 - near_side
    build(far_ref, (2 * side - 1) * CLON, (side,), table, wt, ln, lc)
    edge_sums = s_edge[...] + dot(wt[...], lc[...], NT)
    for pair in range(2):
        rows = slice(pair * 256, (pair + 1) * 256)
        s_far[:, rows] = dot(wt[...], ln[0, rows, :], NT)
    for i in range(EXT):
        rows = slice(i * SLOT, (i + 1) * SLOT)
        for k in range(INSTR):
            lanes = slice(k * 128, (k + 1) * 128)
            slot = slice(i * 128 + k * SLOT, i * 128 + (k + 1) * SLOT)
            far = features_of(s_far[rows, lanes] + s_own[side, rows, lanes])
            near = f_near[slot, :]
            feat[slot, 0:128] = jnp.where(near_side == 0, near, far)
            feat[slot, 128:256] = jnp.where(near_side == 0, far, near)

    w1 = w1_ref[...]
    b1 = b1_ref[...]
    edge_feat = edge_features(edge_sums)
    products = [dot(w1[:, a * 128 : (a + 1) * 128], edge_feat) for a in range(3)]
    terms = edge_terms(products)
    pre = b1
    for a in range(3):
        for b in range(3):
            part = products[a][b * CHANNELS : (b + 1) * CHANNELS]
            shift = (EDGE * a + b - 1) % 128
            pre = pre + (part if shift == 0 else pltpu.roll(part, 128 - shift, 1))
    lane_row = lax.broadcasted_iota(jnp.int32, (CHANNELS, 128), 1) // EDGE + lat_first - 1
    inside = (lane_row >= 0) & (lane_row < NLAT)
    edge_hid = jnp.where(inside, silu(pre), 0.0).astype(jnp.bfloat16)
    for h in range(HID):
        y = dot(w1, feat[h * 128 : (h + 3) * 128, :])
        row = lat_first - 1 + h
        for n, half in enumerate(row_total(y, terms, h, b1)):
            act = silu(half)
            if h in (0, HID - 1):
                act = jnp.where((row >= 0) & (row < NLAT), act, 0.0)
            hid[h * CHANNELS : (h + 1) * CHANNELS, n * 128 : (n + 1) * 128] = act.astype(jnp.bfloat16)

    w2 = w2_ref[...]
    b2 = b2_ref[...]
    terms = edge_terms([dot(w2_taps[a], edge_hid) for a in range(3)])
    size = CHANNELS * STEP
    for r in range(CLAT):
        y = dot(w2, hid[r * CHANNELS : (r + 3) * CHANNELS, :])
        for n, half in enumerate(row_total(y, terms, r, b2)):
            stage[pl.ds(n * size + r, CHANNELS, STEP), :] = half

    copies = []
    step = CHANNELS // PARTS
    for part in range(PARTS):
        channels = slice(part * step, (part + 1) * step)
        for n in range(2):
            for p in range(part * step, (part + 1) * step):
                result[p, :, n * 128 : (n + 1) * 128] = stage[
                    n * size + p * STEP : n * size + p * STEP + CLAT, :
                ].astype(jnp.bfloat16)
        copies.append(
            pltpu.make_async_copy(result.at[channels], out_ref.at[channels], sems.at[part])
        )
        copies[-1].start()
    for copy in copies:
        copy.wait()


def encode(near, own, far, w1, w2, w2_taps, b1, b2, table):
    vmem = pl.BlockSpec(memory_space=pltpu.VMEM)
    bf16, f32 = jnp.bfloat16, jnp.float32
    rows = EXT * SLOT
    s_own, s_edge = pl.pallas_call(
        own_kernel,
        out_shape=[
            jax.ShapeDtypeStruct((2, rows, INSTR * 128), f32),
            jax.ShapeDtypeStruct((rows, 128), f32),
        ],
        in_specs=[vmem] * 2,
        out_specs=[vmem] * 2,
        scratch_shapes=[
            pltpu.VMEM((rows, BAND), bf16),
            pltpu.VMEM((2, INSTR * 128, BAND), bf16),
            pltpu.VMEM((128, BAND), bf16),
        ],
        compiler_params=pltpu.CompilerParams(vmem_limit_bytes=16 * 1024 * 1024),
        cost_estimate=pl.CostEstimate(flops=2 * rows * BAND * 1152, bytes_accessed=3000000, transcendentals=0),
    )(own, table)
    f_near, s_edge = pl.pallas_call(
        near_kernel,
        out_shape=[
            jax.ShapeDtypeStruct((EXT * 128, 128), bf16),
            jax.ShapeDtypeStruct((rows, 128), f32),
        ],
        in_specs=[vmem] * 4,
        out_specs=[vmem] * 2,
        scratch_shapes=[
            pltpu.VMEM((rows, BAND), bf16),
            pltpu.VMEM((1, INSTR * 128, BAND), bf16),
            pltpu.VMEM((128, BAND), bf16),
            pltpu.VMEM((rows, INSTR * 128), f32),
        ],
        compiler_params=pltpu.CompilerParams(vmem_limit_bytes=16 * 1024 * 1024),
        cost_estimate=pl.CostEstimate(flops=2 * rows * BAND * 640, bytes_accessed=3000000, transcendentals=0),
    )(near, table, s_own, s_edge)
    return pl.pallas_call(
        encode_kernel,
        out_shape=jax.ShapeDtypeStruct((CHANNELS, CLAT, CLON), bf16),
        in_specs=[vmem] * 10,
        out_specs=pl.BlockSpec(memory_space=pl.ANY),
        scratch_shapes=[
            pltpu.VMEM((rows, BAND), bf16),
            pltpu.VMEM((1, INSTR * 128, BAND), bf16),
            pltpu.VMEM((128, BAND), bf16),
            pltpu.VMEM((rows, INSTR * 128), f32),
            pltpu.VMEM((EXT * 128, CLON), bf16),
            pltpu.VMEM((HID * CHANNELS, CLON), bf16),
            pltpu.VMEM((2 * CHANNELS * STEP, 128), f32),
            pltpu.VMEM((CHANNELS, CLAT, CLON), bf16),
            pltpu.SemaphoreType.DMA((PARTS,)),
        ],
        compiler_params=pltpu.CompilerParams(vmem_limit_bytes=24 * 1024 * 1024),
    )(far, table, s_own, s_edge, f_near, w1, w2, w2_taps, b1, b2)


def along(array, shape):
    return lax.broadcast_in_dim(array, shape, (len(shape) - 1,))


def pack(obs_values, obs_lat, obs_lon, instrument):
    shape = (SLOT, ROWS_DEV)
    row = lax.broadcasted_iota(jnp.int32, shape, 0)
    high = jnp.where(row == 0, along(obs_lat, shape), 0)
    ints = jnp.where(row == 31, along(obs_lon, shape), 0)
    ints = jnp.where(row == 0, along(instrument, shape), ints)
    return jnp.pad(obs_values, ((1, 1), (0, 0))) + (high * INSTR + ints).astype(jnp.float32)


def pack_small(b_first, b_second, scale):
    shape = (8, CHANNELS)
    row = lax.broadcasted_iota(jnp.int32, shape, 0)
    small = jnp.where(row == 2, along(scale, shape), 0.0)
    small = jnp.where(row == 1, along(b_second, shape), small)
    return jnp.where(row == 0, along(b_first, shape), small)


def arrange(w_first, w_second, small):
    bf16, f32 = jnp.bfloat16, jnp.float32
    wide = jnp.pad(w_second, ((0, 0), (0, 0), (CHANNELS, 0), (0, CIN - CHANNELS)))
    both = jnp.pad(w_first, ((0, 0), (0, 0), (0, CHANNELS), (0, 0))) + wide
    return pl.pallas_call(
        weights_kernel,
        out_shape=[
            jax.ShapeDtypeStruct((3 * CHANNELS, 3 * 128), bf16),
            jax.ShapeDtypeStruct((3 * CHANNELS, 3 * CHANNELS), bf16),
            jax.ShapeDtypeStruct((3, 3 * CHANNELS, CHANNELS), bf16),
            jax.ShapeDtypeStruct((CHANNELS, 1), f32),
            jax.ShapeDtypeStruct((CHANNELS, 1), f32),
            jax.ShapeDtypeStruct((2 * INSTR, 128), f32),
        ],
        in_specs=[pl.BlockSpec(memory_space=pltpu.VMEM)] * 2,
        out_specs=[pl.BlockSpec(memory_space=pltpu.VMEM)] * 6,
        compiler_params=pltpu.CompilerParams(vmem_limit_bytes=4 * 1024 * 1024),
        cost_estimate=pl.CostEstimate(flops=20000000, bytes_accessed=1000000, transcendentals=0),
    )(both, small)


def send(array, axis, target):
    peers = lax.axis_size(axis)
    return lax.ppermute(array, axis, [(i, target(i) % peers) for i in range(peers)])


def body(
    obs_values, obs_lat, obs_lon, instrument, length_scale, w_first, b_first, w_second, b_second
):
    rows = pack(obs_values, obs_lat, obs_lon, instrument)
    rows, length_scale = lax.optimization_barrier((rows, length_scale))
    scale = jnp.pad(length_scale, (0, CHANNELS - INSTR))
    others = send(rows, "lat", lambda i: i ^ 1)
    rows, others, scale, b_first, b_second, w_first, w_second = lax.optimization_barrier(
        (rows, others, scale, b_first, b_second, w_first, w_second)
    )
    rows = jnp.concatenate([rows, others], axis=1)
    rows, b_first, b_second, w_first, w_second = lax.optimization_barrier(
        (rows, b_first, b_second, w_first, w_second)
    )
    weights = arrange(w_first, w_second, pack_small(b_first, b_second, scale))
    others = send(rows, "lat", lambda i: i ^ 3)
    rows, others, weights = lax.optimization_barrier((rows, others, weights))
    rows = jnp.concatenate([rows, others], axis=1)
    across = send(rows, "lat", lambda i: i ^ 8)
    beside = send(rows, "lat", lambda i: i + 4 if i % 2 == 0 else i - 4)
    others = [across, send(beside, "lat", lambda i: i ^ 1), beside]
    rows = jnp.stack([rows] + others)
    near = send(rows, "lon", lambda i: i ^ 1)
    far = send(rows, "lon", lambda i: ((i + 1) ^ 1) - 1)
    return encode(near, rows, far, *weights)


def solution(mesh):
    return jax.shard_map(
        body,
        mesh=mesh,
        in_specs=(
            P(None, ("lat", "lon")),
            P(("lat", "lon")),
            P(("lat", "lon")),
            P(("lat", "lon")),
            P(),
            P(),
            P(),
            P(),
            P(),
        ),
        out_specs=P(None, "lat", "lon"),
        check_vma=False,
    )
```
